32 devices in a mesh: region: 8 (over z, x), sub: 4 (over y, core).
Axes of the slice: x: 2, y: 2, z: 4, core: 2. Of those that a mesh axis runs over, the one named last changes fastest.
Arguments:
- kkt_inverse: bfloat16 [65536, 2048], P(('region', 'sub')), may hold values from -0.125 to 0.125
- cost_terms: bfloat16 [65536, 256], P(('region', 'sub')), may hold values from -6 to 6
- dual_start: float32 [49152, 256], P(('region', 'sub')), may hold values from -4 to 4
- consensus_start: float32 [8192, 256], P(('region', 'sub')), may hold values from -6 to 6
- block_target: int32 [32, 12], P(('region', 'sub')), may hold values from -1 to 15, as said below
Outputs:
- state: float32 [65536, 256], P(('region', 'sub'))
- duals: float32 [49152, 256], P(('region', 'sub'))
- consensus: float32 [8192, 256], P(('region', 'sub'))
- norms: float32 [2, 2], replicated
The draws below stay inside these ranges and needn't reach their ends.
Inputs may be any that keep to these rules, and one draw needn't show every extreme that they name: `block_target`: A device has at most 2 live blocks bound for one region, and every device has exactly 2 for some region. At least 10 of a device's slots are live; some device has all 12 live.
All inputs are finite; a program needn't handle non-finite values.
Results may differ from the reference program's by a relative error of at most 0.0034.
Values sent between devices are 32-bit elements; how exact they have to be, the bound alone decides.
No kernel may reach another device: no remote copies, remote signals or barrier semaphores. Data moves between devices by JAX's collectives and lax.ppermute only.
A program may use at most 128 MiB of HBM per device.

```python
import jax
import jax.numpy as jnp
from jax import lax

K = 2048
BLOCK = 128
S = 256
NB = 12
OWNB = 2
CAP = 2
ITERS = 2
N_REGION = 8
N_SUB = 4
DEVICES = 32


def draw_block_target(key, part):
    slots = N_REGION * CAP
    full_device = jax.random.randint(jax.random.fold_in(key, 7), (), 0, DEVICES)

    def one_device(index):
        dkey = jax.random.fold_in(jax.random.fold_in(key, 11), index)
        keys = jax.random.split(dkey, 5)
        first = jax.random.randint(keys[0], (), 0, N_REGION)
        order = jax.random.permutation(keys[1], slots)
        positions = jnp.arange(slots, dtype=jnp.int32)
        peer_of = positions // CAP
        score = jnp.where(peer_of == first, positions % CAP - CAP, order)
        chosen = jnp.argsort(score, stable=True)[:NB]
        peers = (chosen // CAP).astype(jnp.int32)
        active = jax.random.randint(keys[2], (), NB - NB // 6, NB + 1)
        active = jnp.where(index == full_device, NB, active)
        alive = jnp.arange(NB, dtype=jnp.int32) < active
        shuffle = jax.random.permutation(keys[3], NB)
        peers = peers[shuffle]
        alive = alive[shuffle]
        owned_index = jax.random.randint(keys[4], (NB,), 0, OWNB)
        return jnp.where(alive, peers * OWNB + owned_index, -1).astype(jnp.int32)
    return jax.vmap(one_device)(jnp.arange(DEVICES, dtype=jnp.int32))


def block_levels(stream_key, dims, shards, low, high):
    gain = 1.0
    for axis_at, shards_of in shards:
        steps = jax.random.uniform(jax.random.fold_in(jax.random.fold_in(stream_key, 6), axis_at), (shards_of,), jnp.float32, low / len(shards), high / len(shards))
        gain = gain * jnp.repeat(jnp.exp(steps), dims[axis_at] // shards_of).reshape((-1,) + (1,) * (len(dims) - 1 - axis_at))
    return gain


def bell_draw(rng, shape, width, reach, pieces=(), kind=jnp.bfloat16):
    values = width * jax.random.normal(rng, shape, jnp.float32)
    if pieces:
        values = values * block_levels(rng, shape, pieces, -0.22, 0.18)
    return jnp.clip(values, -reach, reach).astype(kind)


def setup_inputs(seed: int = 0) -> dict:
    arg_keys = jax.random.split(jax.random.key(seed), 6)
    return {
        "kkt_inverse": bell_draw(arg_keys[0], (DEVICES * K, K), K ** -0.5, 0.125, ((0, 32),)),
        "cost_terms": bell_draw(arg_keys[1], (DEVICES * K, S), 1.0, 6.0, ((0, 32),)),
        "dual_start": bell_draw(arg_keys[2], (DEVICES * NB * BLOCK, S), 0.5, 4.0, ((0, 32),), jnp.float32),
        "consensus_start": bell_draw(arg_keys[3], (DEVICES * OWNB * BLOCK, S), 1.0, 6.0, ((0, 32),), jnp.float32),
        "block_target": draw_block_target(jax.random.fold_in(arg_keys[5], 71), 0),
    }


penalty = 1.5

def reference(kkt_inverse, cost_terms, dual_start, consensus_start, block_target):
    highest = lax.Precision.HIGHEST
    bound_rows = NB * BLOCK
    inverse = kkt_inverse.reshape(DEVICES, K, K)
    cost = cost_terms.reshape(DEVICES, K, S)
    base = lax.map(lambda pair: jnp.dot(pair[0], pair[1], preferred_element_type=jnp.float32), (inverse, cost))
    device = jnp.arange(DEVICES, dtype=jnp.int32)
    sub_index = device % N_SUB
    live = block_target >= 0
    livef = live.astype(jnp.float32)
    owner = block_target // OWNB * N_SUB + sub_index[:, None]
    slot = jnp.where(live, owner * OWNB + block_target % OWNB, -1)
    onehot = (slot[:, :, None] == jnp.arange(DEVICES * OWNB, dtype=jnp.int32)[None, None, :]).astype(jnp.float32)
    counts = lax.optimization_barrier(jnp.sum(onehot, axis=(0, 1)))
    floor_counts = jnp.maximum(counts, 1.0)
    dual = dual_start.reshape(DEVICES, NB, BLOCK * S)
    cons = consensus_start.reshape(DEVICES * OWNB, BLOCK * S)

    def fetch(values):
        return jnp.einsum('dng,gm->dnm', onehot, values, precision=highest)

    def couple(pair):
        return jnp.dot(pair[0][:, :bound_rows], pair[1], preferred_element_type=jnp.float32)
    fetched = fetch(cons)
    rows = []
    field = base
    for step in range(ITERS):
        drive = (penalty * livef[:, :, None] * (fetched - dual)).reshape(DEVICES, bound_rows, S).astype(jnp.bfloat16)
        field = base + lax.map(couple, (inverse, drive))
        copies = field[:, :bound_rows].reshape(DEVICES, NB, BLOCK * S)
        sums = jnp.einsum('dng,dnm->gm', onehot, copies + dual, precision=highest)
        renewed = sums / floor_counts[:, None]
        fetched = fetch(renewed)
        gap = copies - fetched
        primal = jnp.sum(livef[:, :, None] * gap * gap)
        change = renewed - cons
        moved = penalty * penalty * jnp.sum(counts[:, None] * change * change)
        dual = dual + livef[:, :, None] * gap
        cons = renewed
        rows.append(jnp.stack([primal, moved]))
    table = jnp.stack(rows)
    norms = jnp.sqrt(table / (DEVICES * S * BLOCK))
    state = field.reshape(DEVICES * K, S)
    return (state, dual.reshape(DEVICES * NB * BLOCK, S), cons.reshape(DEVICES * OWNB * BLOCK, S), norms)
```

```python
import jax
import jax.numpy as jnp
from jax import lax
from jax.experimental import pallas as pl
from jax.experimental.pallas import tpu as pltpu
from jax.sharding import PartitionSpec as P

BLOCK = 128
CAP = 2
ITERS = 2
HALVES = 2
TILE = 8


penalty = 1.5

VMEM = pl.BlockSpec(memory_space=pltpu.VMEM)
SMEM = pl.BlockSpec(memory_space=pltpu.SMEM)
ANY = pl.BlockSpec(memory_space=pl.ANY)


def grid_of(peers):
    columns = 1
    while (2 * columns) ** 2 <= peers:
        columns *= 2
    return peers // columns, columns


def ring_place(region, peers):
    rows, columns = grid_of(peers)
    row, column = region // columns, region % columns
    up = rows - 1 - row
    if columns == 1:
        return row
    right = up % 2 == 0
    if isinstance(region, int):
        if column == 0:
            return row
        return rows + up * (columns - 1) + (column - 1 if right else columns - 1 - column)
    along = jnp.where(right, column - 1, columns - 1 - column)
    return jnp.where(column == 0, row, rows + up * (columns - 1) + along)


def f32(*shape):
    return jax.ShapeDtypeStruct(shape, jnp.float32)


def call(body, name, ins, in_specs, outs, out_specs, scratch=(), aliases=None, flops=0, moved=1 << 20):
    return pl.pallas_call(
        body,
        name=name,
        out_shape=outs,
        in_specs=in_specs,
        out_specs=out_specs,
        scratch_shapes=scratch,
        input_output_aliases=aliases or {},
        cost_estimate=pl.CostEstimate(flops=flops, bytes_accessed=moved, transcendentals=0),
        compiler_params=pltpu.CompilerParams(vmem_limit_bytes=16 << 20),
    )(*ins)


def prepare(region, target, cons, peers):
    rows, scen = cons.shape
    blocks = target.shape[1]
    owned = rows // BLOCK
    width = scen // HALVES

    def body(region_ref, target_ref, cons_ref, table_ref, *half_refs):
        here = ring_place(region_ref[0], peers)
        for i in range(2 * CAP * peers):
            table_ref[i] = -1
        for j in range(blocks):
            t = target_ref[0, j]

            @pl.when(t >= 0)
            def _(t=t, j=j):
                owner = t // owned
                ahead = ring_place(owner, peers) - here
                ahead = jnp.where(ahead < 0, ahead + peers, ahead)
                first = CAP * ahead
                at = first + jnp.where(table_ref[first] >= 0, 1, 0)
                table_ref[at] = j
                table_ref[CAP * peers + at] = t - owner * owned

        for h, ref in enumerate(half_refs):
            ref[...] = cons_ref[:, h * width : (h + 1) * width]

    out = call(
        body,
        "prepare",
        (region, target, cons),
        [SMEM, SMEM, VMEM],
        [jax.ShapeDtypeStruct((2 * CAP * peers,), jnp.int32)] + [f32(rows, width)] * HALVES,
        [SMEM] + [VMEM] * HALVES,
    )
    return out[0], out[1:]


def base_product(kkt, cost):
    rows, scen = kkt.shape[0], cost.shape[1]
    step = 256

    def body(kkt_ref, cost_ref, out_ref):
        @pl.loop(0, rows // step)
        def _(i):
            at = pl.ds(pl.multiple_of(i * step, step), step)
            out_ref[at, :] = jnp.dot(kkt_ref[at, :], cost_ref[...], preferred_element_type=jnp.float32)

    return call(
        body, "base_product", (kkt, cost), [VMEM] * 2, f32(rows, scen), VMEM, flops=2 * rows * rows * scen, moved=12 << 20
    )


def slots_of(table_ref, peers):
    def each(do):
        for r in range(peers):
            for c in range(CAP):
                j = table_ref[CAP * r + c]

                @pl.when(j >= 0)
                def _(r=r, c=c, j=j):
                    b = table_ref[CAP * peers + CAP * r + c]
                    slot = pl.ds(pl.multiple_of(j * BLOCK, BLOCK), BLOCK)
                    block = pl.ds(pl.multiple_of(b * BLOCK, BLOCK), BLOCK)
                    do(r, slot, block)

    return each


def fold(x):
    return jnp.sum(x.reshape(-1, TILE, x.shape[-1]), axis=0)


def first_solve(h, table, pieces, dual, base, kkt, owned, counting):
    peers = len(pieces)
    bound, scen = dual.shape
    width = scen // HALVES
    cols = slice(h * width, (h + 1) * width)
    own = owned * BLOCK
    sent = own + (TILE if counting else 0)
    step = 512 if bound % 512 == 0 else BLOCK

    def body(*refs):
        table_ref, refs = refs[0], refs[1:]
        piece, (dual_ref, base_ref, kkt_ref, z_ref), refs = refs[:peers], refs[peers : peers + 4], refs[peers + 4 :]
        part, (drive_ref,) = refs[:peers], refs[peers:]
        each = slots_of(table_ref, peers)
        drive_ref[...] = jnp.zeros_like(drive_ref)

        def driven(r, slot, block):
            drive_ref[slot, :] = (penalty * (piece[r][block, :] - dual_ref[slot, cols])).astype(jnp.bfloat16)

        each(driven)

        @pl.loop(0, bound // step)
        def _(i):
            at = pl.ds(pl.multiple_of(i * step, step), step)
            got = jnp.dot(kkt_ref[at, :bound], drive_ref[...], preferred_element_type=jnp.float32)
            z_ref[at, :] = (base_ref[at, cols] + got) + dual_ref[at, cols]

        for r in range(peers):
            part[r][:own, :] = jnp.zeros((own, width), jnp.float32)
            if counting:
                row = lax.broadcasted_iota(jnp.int32, (TILE, width), 0)
                count = jnp.zeros((TILE, width), jnp.float32)
                for c in range(CAP):
                    b = table_ref[CAP * peers + CAP * r + c]
                    count = count + jnp.where(row == b, 1.0, 0.0)
                part[r][own:, :] = count

        def summed(r, slot, block):
            part[r][block, :] += z_ref[slot, :]

        each(summed)

    out = call(
        body,
        "first_solve",
        (table, *pieces, dual, base, kkt),
        [SMEM] + [VMEM] * (peers + 3),
        [f32(bound, width)] + [f32(sent, width)] * peers,
        [VMEM] * (1 + peers),
        [pltpu.VMEM((bound, width), jnp.bfloat16)],
        flops=2 * bound * bound * width,
        moved=8 << 20,
    )
    return out[0], out[1:]


def second_solve(h, table, pieces, z, dual, base, kkt, owned, state):
    peers = len(pieces)
    bound, scen = dual.shape
    rows = base.shape[0]
    width = scen // HALVES
    cols = slice(h * width, (h + 1) * width)
    own = owned * BLOCK
    step = 512 if rows % 512 == 0 else BLOCK
    given = 0 if state is None else 1

    def body(*refs):
        table_ref, refs = refs[0], refs[1:]
        piece, (z_ref, dual_ref, base_ref, kkt_ref), refs = refs[:peers], refs[peers : peers + 4], refs[peers + 4 + given :]
        state_ref, next_ref, norm_ref, refs = refs[0], refs[1], refs[2], refs[3:]
        part, (drive_ref, field_ref, sem) = refs[:peers], refs[peers:]
        each = slots_of(table_ref, peers)
        drive_ref[...] = jnp.zeros_like(drive_ref)
        norm_ref[...] = jnp.zeros_like(norm_ref)
        next_ref[...] = dual_ref[:, cols]

        def driven(r, slot, block):
            fetched = piece[r][block, :]
            renewed_dual = z_ref[slot, :] - fetched
            gap = renewed_dual - dual_ref[slot, cols]
            norm_ref[:TILE, :] += fold(gap * gap)
            next_ref[slot, :] = renewed_dual
            drive_ref[slot, :] = (penalty * (fetched - renewed_dual)).astype(jnp.bfloat16)

        each(driven)

        def store(i):
            at = pl.ds(pl.multiple_of(i * step, step), step)
            return pltpu.make_async_copy(field_ref.at[at, :], state_ref.at[at, cols], sem.at[i])

        for i in range(rows // step):
            at = pl.ds(i * step, step)
            got = jnp.dot(kkt_ref[at, :bound], drive_ref[...], preferred_element_type=jnp.float32)
            field_ref[at, :] = base_ref[at, cols] + got
            store(i).start()
        for r in range(peers):
            part[r][...] = jnp.zeros((own, width), jnp.float32)

        def summed(r, slot, block):
            copies = field_ref[slot, :]
            shift = copies - piece[r][block, :]
            norm_ref[TILE:, :] += fold(shift * shift)
            total = copies + next_ref[slot, :]
            next_ref[slot, :] = total
            part[r][block, :] += total

        each(summed)
        for i in range(rows // step):
            store(i).wait()

    before = () if state is None else (state,)
    out = call(
        body,
        "second_solve",
        (table, *pieces, z, dual, base, kkt, *before),
        [SMEM] + [VMEM] * (peers + 4) + [ANY] * given,
        [f32(rows, scen), f32(bound, width), f32(2 * TILE, width)] + [f32(own, width)] * peers,
        [ANY] + [VMEM] * (2 + peers),
        [
            pltpu.VMEM((bound, width), jnp.bfloat16),
            pltpu.VMEM((rows, width), jnp.float32),
            pltpu.SemaphoreType.DMA((rows // step,)),
        ],
        aliases={peers + 5: 0} if given else None,
        flops=2 * bound * rows * width,
        moved=10 << 20,
    )
    return out[0], out[1], out[2], out[3:]


def add_pairs(pairs):
    def body(*refs):
        for i in range(len(pairs)):
            refs[2 * len(pairs) + i][...] = refs[2 * i][...] + refs[2 * i + 1][...]

    out = call(
        body,
        "add_pairs",
        tuple(x for pair in pairs for x in pair),
        [VMEM] * (2 * len(pairs)),
        [f32(*pair[0].shape) for pair in pairs],
        [VMEM] * len(pairs),
    )
    return list(out)


def renew(parts, before, count, norms):
    own, width = before.shape
    owned = own // BLOCK
    counted = count is None

    def body(*refs):
        parts_ref, refs = refs[: len(parts)], refs[len(parts) :]
        before_ref, refs = refs[0], refs[1:]
        if not counted:
            count_ref, refs = refs[0], refs[1:]
        norm_refs, refs = refs[: len(norms)], refs[len(norms) :]
        new_ref, moved_ref = refs[0], refs[1]

        def total(at):
            value = parts_ref[0][at, :]
            for ref in parts_ref[1:]:
                value = value + ref[at, :]
            return value

        if counted:
            tile = total(slice(own, own + TILE))
            refs[2][...] = tile
        else:
            tile = count_ref[...]
        moved = jnp.zeros((TILE, width), jnp.float32)
        for b in range(owned):
            at = slice(b * BLOCK, (b + 1) * BLOCK)
            many = tile[b : b + 1, :]
            value = total(at) / jnp.maximum(many, 1.0)
            change = value - before_ref[at, :]
            moved = moved + many * fold(change * change)
            new_ref[at, :] = value
        moved_ref[...] = moved
        if norms:
            first = norm_refs[0][...] + norm_refs[1][...]
            sums = [
                first[:TILE, :],
                norm_refs[2][...] + norm_refs[3][...],
                first[TILE:, :],
                norm_refs[4][...] + moved,
            ]
            row = lax.broadcasted_iota(jnp.int32, (TILE, width), 0)
            block = jnp.zeros((TILE, width), jnp.float32)
            for i, x in enumerate(sums):
                block = jnp.where(row == i, jnp.sum(x, axis=0, keepdims=True), block)
            new_ref[own:, :] = block

    ins = (*parts, before) + (() if counted else (count,)) + tuple(norms)
    outs = [f32(own + (TILE if norms else 0), width), f32(TILE, width)] + ([f32(TILE, width)] if counted else [])
    return call(body, "renew", ins, [VMEM] * len(ins), outs, [VMEM] * len(outs))


def finish(h, table, pieces, z, scen, owned, outputs):
    peers = len(pieces)
    bound, width = z.shape
    cols = slice(h * width, (h + 1) * width)
    own = owned * BLOCK
    given = len(outputs)

    def body(*refs):
        table_ref, refs = refs[0], refs[1:]
        piece, z_ref, refs = refs[:peers], refs[peers], refs[peers + 1 + given :]
        dual_ref, cons_ref, new_ref, sem = refs
        kept = pltpu.make_async_copy(piece[0].at[:own, :], cons_ref.at[:, cols], sem.at[0])
        kept.start()
        each = slots_of(table_ref, peers)
        new_ref[...] = z_ref[...]

        def renewed(r, slot, block):
            new_ref[slot, :] = z_ref[slot, :] - piece[r][block, :]

        each(renewed)
        out = pltpu.make_async_copy(new_ref, dual_ref.at[:, cols], sem.at[1])
        out.start()
        out.wait()
        kept.wait()

    return call(
        body,
        "finish",
        (table, *pieces, z, *outputs),
        [SMEM] + [VMEM] * (peers + 1) + [ANY] * given,
        [f32(bound, scen), f32(own, scen)],
        [ANY] * 2,
        [pltpu.VMEM((bound, width), jnp.float32), pltpu.SemaphoreType.DMA((2,))],
        aliases={peers + 2: 0, peers + 3: 1} if given else None,
        moved=3 << 20,
    )


def sum_tails(pieces, own):
    width = pieces[0].shape[1]

    def body(*refs):
        total = refs[0][own:, :]
        for ref in refs[1:-1]:
            total = total + ref[own:, :]
        refs[-1][...] = total

    return call(body, "sum_tails", tuple(pieces), [VMEM] * len(pieces), f32(TILE, width), VMEM)


def norm_table(tiles, scale):
    def body(*refs):
        total = refs[0][...]
        for ref in refs[1:-1]:
            total = total + ref[...]
        total = jnp.sum(total, axis=1, keepdims=True)
        row = lax.broadcasted_iota(jnp.int32, (ITERS, 2), 0)
        col = lax.broadcasted_iota(jnp.int32, (ITERS, 2), 1)
        primal = jnp.where(row == 0, total[0:1, :], total[2:3, :] - total[3:4, :])
        moved = penalty * penalty * jnp.where(row == 0, total[1:2, :], total[3:4, :])
        refs[-1][...] = jnp.sqrt(jnp.maximum(jnp.where(col == 0, primal, moved), 0.0) / scale)

    return call(body, "norm_table", tuple(tiles), [VMEM] * len(tiles), f32(ITERS, 2), VMEM)


def shards(kkt, cost, dual, cons, target):
    scen = cost.shape[1]
    owned = cons.shape[0] // BLOCK
    peers = lax.axis_size("region")
    subs = lax.axis_size("sub")
    order = sorted(range(peers), key=lambda region: ring_place(region, peers))
    ahead = [(order[i], order[(i + 1) % peers]) for i in range(peers)]
    behind = [(b, a) for a, b in ahead]

    def forward(x):
        return lax.ppermute(x, "region", ahead)

    def backward(x):
        return lax.ppermute(x, "region", behind)

    def reach(h):
        long, short = peers // 2, (peers - 1) // 2
        return (long, short) if h % 2 == 0 else (short, long)

    def gather(h, piece):
        far, near = reach(h)
        pieces = [piece] * peers
        f = b = piece
        for k in range(1, max(far, near) + 1):
            if k <= far:
                f = pieces[(peers - k) % peers] = forward(f)
            if k <= near:
                b = pieces[k] = backward(b)
        return pieces

    def scatter(h, parts):
        far, near = reach(h)
        f, b = parts[far], parts[peers - near]
        for k in range(1, max(far, near) + 1):
            pairs = []
            if k <= far:
                f = forward(f)
            if k <= near:
                b = backward(b)
            if k < far:
                pairs.append((f, parts[far - k]))
            if k < near:
                pairs.append((b, parts[peers - near + k]))
            if pairs:
                added = add_pairs(pairs)
                if k < far:
                    f = added.pop(0)
                if k < near:
                    b = added.pop(0)
        return [parts[0], f, b]

    region = lax.axis_index("region").astype(jnp.int32).reshape(1)
    table, halves = prepare(region, target, cons, peers)
    base = base_product(kkt, cost)
    state, outputs = None, ()
    every = range(HALVES)
    pieces = [gather(h, halves[h]) for h in every]
    count = None
    z, renewed, moved1, moved2, gaps = {}, {}, {}, {}, {}
    for h in every:
        z[h], parts = first_solve(h, table, pieces[h], dual, base, kkt, owned, count is None)
        out = renew(scatter(h, parts), halves[h], count, ())
        renewed[h], moved1[h] = out[0], out[1]
        if count is None:
            count = out[2]
        pieces[h] = gather(h, renewed[h])
    for h in every:
        state, z[h], gaps[h], parts = second_solve(h, table, pieces[h], z[h], dual, base, kkt, owned, state)
        norms = (gaps[0], gaps[1], moved1[0], moved1[1], moved2[0]) if h == HALVES - 1 else ()
        out = renew(scatter(h, parts), renewed[h], count, norms)
        moved2[h] = out[1]
        pieces[h] = gather(h, out[0])
    tail = sum_tails(pieces[HALVES - 1], owned * BLOCK)
    turns = [lax.ppermute(tail, "sub", [(i, (i + k) % subs) for i in range(subs)]) for k in range(1, subs)]
    for h in every:
        outputs = finish(h, table, pieces[h], z[h], scen, owned, outputs)
    norms = norm_table([tail, *turns], float(peers * subs * scen * BLOCK))
    return (state, outputs[0], outputs[1], norms)


def solution(mesh):
    spec = P(("region", "sub"), None)
    return jax.shard_map(
        shards, mesh=mesh, in_specs=(spec,) * 5, out_specs=(spec, spec, spec, P()), check_vma=False
    )
```

```python
import math

import jax
import jax.numpy as jnp
from jax import lax
from jax.experimental import pallas as pl
from jax.experimental.pallas import tpu as pltpu
from jax.sharding import PartitionSpec as P

BLOCK = 128
CAP = 2
ITERS = 2
HALVES = 2
TILE = 8
LEAD = 1
BASE_AT = {2: 1, 3: 3}
CUTS = 8


penalty = 1.5

VMEM = pl.BlockSpec(memory_space=pltpu.VMEM)
SMEM = pl.BlockSpec(memory_space=pltpu.SMEM)
HBM = pl.BlockSpec(memory_space=pltpu.HBM)


def grid_of(peers):
    columns = 1
    while (2 * columns) ** 2 <= peers:
        columns *= 2
    return peers // columns, columns


def ring_place(region, peers):
    rows, columns = grid_of(peers)
    row, column = region // columns, region % columns
    up = rows - 1 - row
    if columns == 1:
        return row
    right = up % 2 == 0
    if isinstance(region, int):
        if column == 0:
            return row
        return rows + up * (columns - 1) + (column - 1 if right else columns - 1 - column)
    along = jnp.where(right, column - 1, columns - 1 - column)
    return jnp.where(column == 0, row, rows + up * (columns - 1) + along)


def f32(*shape):
    return jax.ShapeDtypeStruct(shape, jnp.float32)


def call(body, name, ins, in_specs, outs, out_specs, scratch=(), aliases=None, flops=0, moved=1 << 20, room=4, pins=()):
    ins = tuple(pltpu.with_memory_space_constraint(x, pltpu.HBM) if spec is HBM else x for x, spec in zip(ins, in_specs))
    many = isinstance(outs, (list, tuple))
    shapes, specs = (list(outs), list(out_specs)) if many else ([outs], [out_specs])
    for i, spec in enumerate(specs):
        if spec is HBM:
            shapes[i] = pltpu.HBM(shapes[i].shape, shapes[i].dtype)
        elif i in pins:
            shapes[i] = pltpu.VMEM(shapes[i].shape, shapes[i].dtype)
    return pl.pallas_call(
        body,
        name=name,
        out_shape=shapes if many else shapes[0],
        in_specs=in_specs,
        out_specs=out_specs,
        scratch_shapes=scratch,
        input_output_aliases=aliases or {},
        cost_estimate=pl.CostEstimate(flops=flops, bytes_accessed=moved, transcendentals=0),
        compiler_params=pltpu.CompilerParams(vmem_limit_bytes=room << 20),
    )(*ins)


def tie(values, others, near=()):
    values, others = list(values), list(others)

    def body(*refs):
        del refs

    out = call(
        body,
        "tie",
        (*values, *others, *near),
        [VMEM] * len(values) + [HBM] * len(others) + [VMEM] * len(near),
        [f32(*x.shape) for x in values],
        [VMEM] * len(values),
        aliases={i: i for i in range(len(values))},
        moved=0,
    )
    return list(out)


class Loads:
    def __init__(self, sem):
        self.sem, self.used, self.flying = sem, 0, {}

    def start(self, name, src, dst):
        copy = pltpu.make_async_copy(src, dst, self.sem.at[self.used])
        copy.start()
        self.used += 1
        self.flying[name] = copy

    def wait(self, name):
        self.flying.pop(name).wait()


def prepare(region, target, cons, kkt, cost, dual, peers):
    blocks = target.shape[1]
    owned = cons.shape[0] // BLOCK
    arrays = (cons, kkt, cost, dual)
    cuts = (1, CUTS, 1, 1)

    def body(region_ref, target_hbm, *refs):
        from_refs, table_ref, to_refs, target_ref, sem = refs[:4], refs[4], refs[5:9], refs[9], refs[10]
        loads = Loads(sem)
        loads.start("target", target_hbm, target_ref)
        for i, (src, dst) in enumerate(zip(from_refs, to_refs)):
            size = src.shape[0] // cuts[i]
            for c in range(cuts[i]):
                at = slice(c * size, (c + 1) * size)
                loads.start((i, c), src.at[at, :], dst.at[at, :])
        here = ring_place(region_ref[0], peers)
        for i in range(2 * CAP * peers):
            table_ref[i] = -1
        loads.wait("target")
        for j in range(blocks):
            t = target_ref[0, j]

            @pl.when(t >= 0)
            def _(t=t, j=j):
                owner = t // owned
                ahead = ring_place(owner, peers) - here
                ahead = jnp.where(ahead < 0, ahead + peers, ahead)
                first = CAP * ahead
                at = first + jnp.where(table_ref[first] >= 0, 1, 0)
                table_ref[at] = j
                table_ref[CAP * peers + at] = t - owner * owned

        for i in range(4):
            for c in range(cuts[i]):
                loads.wait((i, c))

    out = call(
        body,
        "prepare",
        (region, target, *arrays),
        [SMEM] + [HBM] * 5,
        [jax.ShapeDtypeStruct((2 * CAP * peers,), jnp.int32)] + [jax.ShapeDtypeStruct(x.shape, x.dtype) for x in arrays],
        [SMEM] + [VMEM] * 4,
        [pltpu.SMEM(target.shape, jnp.int32), pltpu.SemaphoreType.DMA((1 + sum(cuts),))],
        moved=12 << 20,
    )
    return out[0], out[1:]


def halve(pieces):
    rows, scen = pieces[0].shape
    width = scen // HALVES

    def body(*refs):
        for h in range(HALVES):
            refs[HALVES + h][...] = refs[h][:, h * width : (h + 1) * width]

    return call(body, "halve", tuple(pieces), [VMEM] * HALVES, [f32(rows, width)] * HALVES, [VMEM] * HALVES)


def columns(ref, h):
    width = ref.shape[1] // HALVES
    return ref.at[:, h * width : (h + 1) * width]


def base_rows(i, step, kkt, cost):
    rows, scen = kkt.shape[0], cost.shape[1]

    def body(kkt_ref, cost_ref, out_ref):
        out_ref[...] = jnp.dot(
            kkt_ref[i * step : (i + 1) * step, :], cost_ref[...], preferred_element_type=jnp.float32
        )

    return call(
        body,
        "base_rows",
        (kkt, cost),
        [VMEM, VMEM],
        f32(step, scen),
        VMEM,
        flops=2 * step * rows * scen,
        moved=3 << 20,
    )


def slots_of(table_ref, peers, blocks):
    out = []
    for r in range(peers):
        row = []
        for c in range(CAP):
            j = table_ref[CAP * r + c]
            b = table_ref[CAP * peers + CAP * r + c]
            read = jnp.maximum(j, 0)
            write = jnp.where(j < 0, blocks, j)
            row.append([pl.ds(pl.multiple_of(x * BLOCK, BLOCK), BLOCK) for x in (read, write, jnp.maximum(b, 0))] + [b])
        out.append(row)
    return out


def fold(x):
    return jnp.sum(x.reshape(-1, TILE, x.shape[-1]), axis=0)


def place(part_ref, totals, slots, owned):
    for o in range(owned):
        value = None
        for total, (_, _, _, b) in zip(totals, slots):
            mine = jnp.where(b == o, total, 0.0)
            value = mine if value is None else value + mine
        part_ref[o * BLOCK : (o + 1) * BLOCK, :] = value


def first_solve(h, table, pieces, dual, bases, kkt, owned, counting):
    peers = len(pieces)
    bound, scen = dual.shape
    width = scen // HALVES
    cols = slice(h * width, (h + 1) * width)
    own = owned * BLOCK
    sent = own + (TILE if counting else 0)
    step = bases[0].shape[0]
    chunks = bound // step

    def body(*refs):
        table_ref, refs = refs[0], refs[1:]
        piece, (dual_ref, kkt_ref), refs = refs[:peers], refs[peers : peers + 2], refs[peers + 2 :]
        piece = [ref if ref.shape[1] == width else columns(ref, h) for ref in piece]
        base_refs, z_ref, refs = refs[:chunks], refs[chunks], refs[chunks + 1 :]
        part, (drive_ref,) = refs[:peers], refs[peers:]
        slots = slots_of(table_ref, peers, bound // BLOCK)
        drive_ref[...] = jnp.zeros_like(drive_ref)
        for r in range(peers):
            for read, write, block, _ in slots[r]:
                drive_ref[write, :] = (penalty * (piece[r][block, :] - dual_ref[read, cols])).astype(jnp.bfloat16)
        for i in range(chunks):
            at = slice(i * step, (i + 1) * step)
            got = jnp.dot(kkt_ref[at, :bound], drive_ref[:bound, :], preferred_element_type=jnp.float32)
            z_ref[at, :] = (base_refs[i][:, cols] + got) + dual_ref[at, cols]
        for r in range(peers):
            place(part[r], [z_ref[read, :] for read, _, _, _ in slots[r]], slots[r], owned)
            if counting:
                row = lax.broadcasted_iota(jnp.int32, (TILE, width), 0)
                count = jnp.zeros((TILE, width), jnp.float32)
                for _, _, _, b in slots[r]:
                    count = count + jnp.where(row == b, 1.0, 0.0)
                part[r][own:, :] = count

    out = call(
        body,
        "first_solve",
        (table, *pieces, dual, kkt, *bases[:chunks]),
        [SMEM] + [VMEM] * (peers + 2 + chunks),
        [f32(bound, width)] + [f32(sent, width)] * peers,
        [VMEM] * (1 + peers),
        [pltpu.VMEM((bound + BLOCK, width), jnp.bfloat16)],
        flops=2 * bound * bound * width,
        moved=8 << 20,
    )
    return out[0], out[1:]


def second_solve(h, table, pieces, z, dual, bases, kkt, owned):
    peers = len(pieces)
    bound, scen = dual.shape
    step = bases[0].shape[0]
    chunks = bound // step
    width = scen // HALVES
    cols = slice(h * width, (h + 1) * width)
    own = owned * BLOCK

    def body(*refs):
        table_ref, refs = refs[0], refs[1:]
        piece, (z_ref, dual_ref, kkt_ref), refs = refs[:peers], refs[peers : peers + 3], refs[peers + 3 :]
        base_refs, refs = refs[:chunks], refs[chunks:]
        field_ref, drive_ref, next_ref, norm_ref, part = refs[0], refs[1], refs[2], refs[3], refs[4:]
        slots = slots_of(table_ref, peers, bound // BLOCK)
        drive_ref[...] = jnp.zeros_like(drive_ref)
        next_ref[:bound, :] = dual_ref[:, cols]
        gaps = jnp.zeros((TILE, width), jnp.float32)
        for r in range(peers):
            for read, write, block, b in slots[r]:
                fetched = piece[r][block, :]
                renewed_dual = z_ref[read, :] - fetched
                gap = renewed_dual - dual_ref[read, cols]
                gaps = gaps + jnp.where(b < 0, 0.0, fold(gap * gap))
                next_ref[write, :] = renewed_dual
                drive_ref[write, :] = (penalty * (fetched - renewed_dual)).astype(jnp.bfloat16)
        for i in range(chunks):
            at = slice(i * step, (i + 1) * step)
            got = jnp.dot(kkt_ref[at, :bound], drive_ref[:bound, :], preferred_element_type=jnp.float32)
            field_ref[at, :] = base_refs[i][:, cols] + got
        shifts = jnp.zeros((TILE, width), jnp.float32)
        for r in range(peers):
            totals = []
            for read, write, block, b in slots[r]:
                copies = field_ref[read, :]
                shift = copies - piece[r][block, :]
                shifts = shifts + jnp.where(b < 0, 0.0, fold(shift * shift))
                totals.append(copies + next_ref[read, :])
            for total, (_, write, _, _) in zip(totals, slots[r]):
                next_ref[write, :] = total
            place(part[r], totals, slots[r], owned)
        norm_ref[:TILE, :] = gaps
        norm_ref[TILE:, :] = shifts

    out = call(
        body,
        "second_solve",
        (table, *pieces, z, dual, kkt, *bases[:chunks]),
        [SMEM] + [VMEM] * (peers + 3 + chunks),
        [
            f32(bound, width),
            jax.ShapeDtypeStruct((bound + BLOCK, width), jnp.bfloat16),
            f32(bound + BLOCK, width),
            f32(2 * TILE, width),
        ]
        + [f32(own, width)] * peers,
        [VMEM] * (4 + peers),
        flops=2 * bound * bound * width,
        moved=8 << 20,
    )
    return out[0], out[1], out[2], out[3], out[4:]


def store_state(h, field, drive, bases, kkt, state):
    bound, width = field.shape
    rows = kkt.shape[0]
    step = bases[0].shape[0]
    cols = slice(h * width, (h + 1) * width)
    given = 0 if state is None else 1
    rest = bases[bound // step :]

    def body(field_ref, drive_ref, kkt_ref, *refs):
        base_refs, (state_hbm, rest_ref, sem) = refs[: len(rest)], refs[len(rest) + given :]
        loads = Loads(sem)
        loads.start("field", field_ref, state_hbm.at[:bound, cols])
        for i in range(len(rest)):
            at = slice(i * step, (i + 1) * step)
            there = slice(bound + i * step, bound + (i + 1) * step)
            got = jnp.dot(kkt_ref[there, :bound], drive_ref[:bound, :], preferred_element_type=jnp.float32)
            rest_ref[at, :] = base_refs[i][:, cols] + got
        loads.start("rest", rest_ref, state_hbm.at[bound:, cols])
        loads.wait("field")
        loads.wait("rest")

    before = () if state is None else (state,)
    return call(
        body,
        "store_state",
        (field, drive, kkt, *rest, *before),
        [VMEM] * (3 + len(rest)) + [HBM] * given,
        f32(rows, HALVES * width),
        HBM,
        [pltpu.VMEM((rows - bound, width), jnp.float32), pltpu.SemaphoreType.DMA((2,))],
        aliases={3 + len(rest): 0} if given else None,
        flops=2 * bound * (rows - bound) * width,
        moved=4 << 20,
    )


def add_pairs(pairs):
    def body(*refs):
        for i in range(len(pairs)):
            refs[2 * len(pairs) + i][...] = refs[2 * i][...] + refs[2 * i + 1][...]

    out = call(
        body,
        "add_pairs",
        tuple(x for pair in pairs for x in pair),
        [VMEM] * (2 * len(pairs)),
        [f32(*pair[0].shape) for pair in pairs],
        [VMEM] * len(pairs),
    )
    return list(out)


def renew(h, parts, before, count, norms):
    own, width = before.shape[0], parts[0].shape[1]
    owned = own // BLOCK
    counted = count is None

    def body(*refs):
        parts_ref, refs = refs[: len(parts)], refs[len(parts) :]
        before_ref, refs = refs[0] if before.shape[1] == width else columns(refs[0], h), refs[1:]
        if not counted:
            count_ref, refs = refs[0], refs[1:]
        norm_refs, refs = refs[: len(norms)], refs[len(norms) :]
        new_ref, moved_ref = refs[0], refs[1]

        def total(at):
            value = parts_ref[0][at, :]
            for ref in parts_ref[1:]:
                value = value + ref[at, :]
            return value

        if counted:
            tile = total(slice(own, own + TILE))
            refs[2][...] = tile
        else:
            tile = count_ref[...]
        moved = jnp.zeros((TILE, width), jnp.float32)
        for b in range(owned):
            at = slice(b * BLOCK, (b + 1) * BLOCK)
            many = tile[b : b + 1, :]
            value = total(at) / jnp.maximum(many, 1.0)
            change = value - before_ref[at, :]
            moved = moved + many * fold(change * change)
            new_ref[at, :] = value
        moved_ref[...] = moved
        if norms:
            gaps = norm_refs[0][...] + norm_refs[3][...]
            sums = [
                gaps[:TILE, :],
                norm_refs[1][...] + norm_refs[4][...],
                gaps[TILE:, :],
                norm_refs[2][...] + moved,
            ]
            row = lax.broadcasted_iota(jnp.int32, (TILE, width), 0)
            block = jnp.zeros((TILE, width), jnp.float32)
            for i, x in enumerate(sums):
                block = jnp.where(row == i, jnp.sum(x, axis=0, keepdims=True), block)
            new_ref[own:, :] = block

    ins = (*parts, before) + (() if counted else (count,)) + tuple(norms)
    outs = [f32(own + (TILE if norms else 0), width), f32(TILE, width)] + ([f32(TILE, width)] if counted else [])
    return call(body, "renew", ins, [VMEM] * len(ins), outs, [VMEM] * len(outs))


def finish(h, table, pieces, z, scen, owned, outputs):
    peers = len(pieces)
    bound, width = z.shape[0] - BLOCK, z.shape[1]
    cols = slice(h * width, (h + 1) * width)
    own = owned * BLOCK
    given = len(outputs)

    def body(*refs):
        table_ref, refs = refs[0], refs[1:]
        piece, z_ref, refs = refs[:peers], refs[peers], refs[peers + 1 + given :]
        dual_hbm, cons_hbm, dual_ref, sem = refs
        loads = Loads(sem)
        loads.start("cons", piece[0].at[:own, :], cons_hbm.at[:, cols])
        dual_ref[:bound, :] = z_ref[:bound, :]
        for r, slots in enumerate(slots_of(table_ref, peers, bound // BLOCK)):
            for read, write, block, _ in slots:
                dual_ref[write, :] = z_ref[read, :] - piece[r][block, :]
        loads.start("dual", dual_ref.at[:bound, :], dual_hbm.at[:, cols])
        loads.wait("dual")
        loads.wait("cons")

    return call(
        body,
        "finish",
        (table, *pieces, z, *outputs),
        [SMEM] + [VMEM] * (peers + 1) + [HBM] * given,
        [f32(bound, scen), f32(own, scen)],
        [HBM] * 2,
        [pltpu.VMEM((bound + BLOCK, width), jnp.float32), pltpu.SemaphoreType.DMA((2,))],
        aliases={peers + 2: 0, peers + 3: 1} if given else None,
        moved=3 << 20,
    )


def sum_tails(pieces, own, done):
    peers, width = len(pieces), pieces[0].shape[1]

    def body(*refs):
        total = refs[0][own:, :]
        for ref in refs[1:peers]:
            total = total + ref[own:, :]
        refs[-1][...] = total

    ins = (*pieces, *done)
    return call(body, "sum_tails", ins, [VMEM] * peers + [HBM] * len(done), f32(TILE, width), VMEM)


def norm_table(tiles, scale):
    def body(*refs):
        total = refs[0][...]
        for ref in refs[1:-1]:
            total = total + ref[...]
        total = jnp.sum(total, axis=1, keepdims=True)
        row = lax.broadcasted_iota(jnp.int32, (ITERS, 2), 0)
        col = lax.broadcasted_iota(jnp.int32, (ITERS, 2), 1)
        primal = jnp.where(row == 0, total[0:1, :], total[2:3, :] - total[3:4, :])
        moved = penalty * penalty * jnp.where(row == 0, total[1:2, :], total[3:4, :])
        refs[-1][...] = jnp.sqrt(jnp.maximum(jnp.where(col == 0, primal, moved), 0.0) / scale)

    return call(body, "norm_table", tuple(tiles), [VMEM] * len(tiles), f32(ITERS, 2), VMEM)


def shards(kkt, cost, dual, cons, target):
    scen = cost.shape[1]
    owned = cons.shape[0] // BLOCK
    peers = lax.axis_size("region")
    subs = lax.axis_size("sub")
    order = sorted(range(peers), key=lambda region: ring_place(region, peers))
    ahead = [(order[i], order[(i + 1) % peers]) for i in range(peers)]
    behind = [(b, a) for a, b in ahead]

    def forward(x):
        return lax.ppermute(x, "region", ahead)

    def backward(x):
        return lax.ppermute(x, "region", behind)

    def reach(h):
        long, short = peers // 2, (peers - 1) // 2
        return (long, short) if h % 2 == 0 else (short, long)

    def gather_all(piece, own, beside):
        across = peers // 2
        pieces = [own] * peers
        f = b = piece
        for k in range(1, across):
            if k > 1:
                f, b = pieces[peers - k + 1], pieces[k - 1] = beside(k, [f, b])
            f, b = pieces[peers - k], pieces[k] = forward(f), backward(b)
        f, b = halve(beside(across, [f, b]))
        return [[*pieces[:across], half, *pieces[across + 1 :]] for half in (forward(f), backward(b))]

    def gather(h, piece, beside=lambda k, x: x):
        far, near = reach(h)
        pieces = [piece] * peers
        f = b = piece
        for k in range(1, max(far, near) + 1):
            values = yield ([f] if k <= far else []) + ([b] if k <= near else [])
            values = beside(k, values)
            if k <= far:
                f = pieces[(peers - k) % peers] = forward(values.pop(0))
            if k <= near:
                b = pieces[k] = backward(values.pop(0))
        return pieces

    def scatter(h, parts):
        far, near = reach(h)
        f, b = parts[far], parts[peers - near]
        for k in range(1, max(far, near) + 1):
            going, coming = f, b
            values = yield ([f] if k <= far else []) + ([b] if k <= near else [])
            f = forward(values.pop(0)) if k <= far else going
            b = backward(values.pop(0)) if k <= near else coming
            pairs = []
            if k < far:
                pairs.append((f, parts[far - k]))
            if k < near:
                pairs.append((b, parts[peers - near + k]))
            if pairs:
                added = add_pairs(pairs)
                if k < far:
                    f = added.pop(0)
                if k < near:
                    b = added.pop(0)
        return [parts[0], f, b]

    region = lax.axis_index("region").astype(jnp.int32).reshape(1)
    table, (own, kkt, cost, dual) = prepare(region, target, cons, kkt, cost, dual, peers)
    step = math.gcd(dual.shape[0], kkt.shape[0])
    chunks = kkt.shape[0] // step
    bases = []

    def beside(k, values):
        some = [own] if k == 2 else []
        while len(bases) < min(chunks, BASE_AT.get(k, chunks if k > 3 else 0)):
            bases.append(base_rows(len(bases), step, kkt, cost))
            some.append(bases[-1])
        return tie(values, [], some) if some else values

    first = gather_all(cons, own, beside)
    known = {"state": None, "outputs": (), "count": None, "norms": []}

    def half(h):
        last = h == HALVES - 1
        pieces = first[h]
        z, parts = first_solve(h, table, pieces, dual, bases, kkt, owned, h == 0)
        arrived = yield from scatter(h, parts)
        out = renew(h, arrived, own, known["count"], ())
        averages, moved = out[0], out[1]
        if known["count"] is None:
            known["count"] = out[2]
        pieces = yield from gather(h, averages)
        field, drive, z, gaps, parts = second_solve(h, table, pieces, z, dual, bases, kkt, owned)
        known["state"] = store_state(h, field, drive, bases, kkt, known["state"])
        arrived = yield from scatter(h, parts)
        norms = known["norms"] + [gaps, moved]
        out = renew(h, arrived, averages, known["count"], norms if last else ())
        known["norms"] = norms + [out[1]]
        pieces = yield from gather(h, out[0])
        if last:
            known["tail"] = sum_tails(pieces, owned * BLOCK, [*known["outputs"], known["state"]])
        known["outputs"] = finish(h, table, pieces, z, scen, owned, known["outputs"])

    turns = [half(h) for h in range(HALVES)]
    waiting = [next(turn) for turn in turns]
    which = LEAD * [0]
    while any(w is not None for w in waiting):
        h = which.pop(0) if which else next_turn(waiting, h)
        values = list(waiting[h])
        try:
            waiting[h] = turns[h].send(values)
        except StopIteration:
            waiting[h] = None
    tail = known["tail"]
    turned = [lax.ppermute(tail, "sub", [(i, (i + k) % subs) for i in range(subs)]) for k in range(1, subs)]
    norms = norm_table([tail, *turned], float(peers * subs * scen * BLOCK))
    return (known["state"], *known["outputs"], norms)


def next_turn(waiting, h):
    for k in range(1, len(waiting) + 1):
        if waiting[(h + k) % len(waiting)] is not None:
            return (h + k) % len(waiting)


def solution(mesh):
    spec = P(("region", "sub"), None)
    return jax.shard_map(
        shards, mesh=mesh, in_specs=(spec,) * 5, out_specs=(spec, spec, spec, P()), check_vma=False
    )
```

```python
import math

import jax
import jax.numpy as jnp
from jax import lax
from jax.experimental import pallas as pl
from jax.experimental.pallas import tpu as pltpu
from jax.sharding import PartitionSpec as P

BLOCK = 128
CAP = 2
ITERS = 2
HALVES = 2
TILE = 8
LEAD = 1
LOAD_TURN = 2
BASE_AT = {4: 2, 6: 4}
CUTS = 8


penalty = 1.5

VMEM = pl.BlockSpec(memory_space=pltpu.VMEM)
SMEM = pl.BlockSpec(memory_space=pltpu.SMEM)
HBM = pl.BlockSpec(memory_space=pltpu.HBM)


def grid_of(peers):
    columns = 1
    while (2 * columns) ** 2 <= peers:
        columns *= 2
    return peers // columns, columns


def ring_place(region, peers):
    rows, columns = grid_of(peers)
    row, column = region // columns, region % columns
    up = rows - 1 - row
    if columns == 1:
        return row
    right = up % 2 == 0
    if isinstance(region, int):
        if column == 0:
            return row
        return rows + up * (columns - 1) + (column - 1 if right else columns - 1 - column)
    along = jnp.where(right, column - 1, columns - 1 - column)
    return jnp.where(column == 0, row, rows + up * (columns - 1) + along)


def f32(*shape):
    return jax.ShapeDtypeStruct(shape, jnp.float32)


def call(body, name, ins, in_specs, outs, out_specs, scratch=(), aliases=None, flops=0, moved=1 << 20, room=4, pins=()):
    ins = tuple(pltpu.with_memory_space_constraint(x, pltpu.HBM) if spec is HBM else x for x, spec in zip(ins, in_specs))
    many = isinstance(outs, (list, tuple))
    shapes, specs = (list(outs), list(out_specs)) if many else ([outs], [out_specs])
    for i, spec in enumerate(specs):
        if spec is HBM:
            shapes[i] = pltpu.HBM(shapes[i].shape, shapes[i].dtype)
        elif i in pins:
            shapes[i] = pltpu.VMEM(shapes[i].shape, shapes[i].dtype)
    return pl.pallas_call(
        body,
        name=name,
        out_shape=shapes if many else shapes[0],
        in_specs=in_specs,
        out_specs=out_specs,
        scratch_shapes=scratch,
        input_output_aliases=aliases or {},
        cost_estimate=pl.CostEstimate(flops=flops, bytes_accessed=moved, transcendentals=0),
        compiler_params=pltpu.CompilerParams(vmem_limit_bytes=room << 20),
    )(*ins)


def tie(values, others, near=()):
    values, others = list(values), list(others)

    def body(*refs):
        del refs

    out = call(
        body,
        "tie",
        (*values, *others, *near),
        [VMEM] * len(values) + [HBM] * len(others) + [VMEM] * len(near),
        [f32(*x.shape) for x in values],
        [VMEM] * len(values),
        aliases={i: i for i in range(len(values))},
        moved=0,
    )
    return list(out)


class Loads:
    def __init__(self, sem):
        self.sem, self.used, self.flying = sem, 0, {}

    def start(self, name, src, dst):
        copy = pltpu.make_async_copy(src, dst, self.sem.at[self.used])
        copy.start()
        self.used += 1
        self.flying[name] = copy

    def wait(self, name):
        self.flying.pop(name).wait()


def split(cons):
    rows, scen = cons.shape
    width = scen // HALVES

    def body(cons_ref, *refs):
        copies = [
            pltpu.make_async_copy(cons_ref.at[:, h * width : (h + 1) * width], refs[h], refs[-1].at[h])
            for h in range(HALVES)
        ]
        for copy in copies:
            copy.start()
        for copy in copies:
            copy.wait()

    return call(
        body, "split", (cons,), [HBM], [f32(rows, width)] * HALVES, [VMEM] * HALVES, [pltpu.SemaphoreType.DMA((HALVES,))]
    )


def prepare(region, target, owned, kkt, cost, dual, peers):
    blocks = target.shape[1]
    arrays = (kkt, cost, dual)
    cuts = (CUTS, 1, 1)

    def body(region_ref, target_hbm, *refs):
        from_refs, table_ref, to_refs, target_ref, sem = refs[:3], refs[3], refs[4:7], refs[7], refs[8]
        loads = Loads(sem)
        loads.start("target", target_hbm, target_ref)
        for i, (src, dst) in enumerate(zip(from_refs, to_refs)):
            size = src.shape[0] // cuts[i]
            for c in range(cuts[i]):
                at = slice(c * size, (c + 1) * size)
                loads.start((i, c), src.at[at, :], dst.at[at, :])
        here = ring_place(region_ref[0], peers)
        for i in range(2 * CAP * peers):
            table_ref[i] = -1
        loads.wait("target")
        for j in range(blocks):
            t = target_ref[0, j]

            @pl.when(t >= 0)
            def _(t=t, j=j):
                owner = t // owned
                ahead = ring_place(owner, peers) - here
                ahead = jnp.where(ahead < 0, ahead + peers, ahead)
                first = CAP * ahead
                at = first + jnp.where(table_ref[first] >= 0, 1, 0)
                table_ref[at] = j
                table_ref[CAP * peers + at] = t - owner * owned

        for i in range(3):
            for c in range(cuts[i]):
                loads.wait((i, c))

    out = call(
        body,
        "prepare",
        (region, target, *arrays),
        [SMEM] + [HBM] * 4,
        [jax.ShapeDtypeStruct((2 * CAP * peers,), jnp.int32)] + [jax.ShapeDtypeStruct(x.shape, x.dtype) for x in arrays],
        [SMEM] + [VMEM] * 3,
        [pltpu.SMEM(target.shape, jnp.int32), pltpu.SemaphoreType.DMA((1 + sum(cuts),))],
        moved=12 << 20,
    )
    return out[0], out[1:]


def halve(pieces):
    rows, scen = pieces[0].shape
    width = scen // HALVES

    def body(*refs):
        for h in range(HALVES):
            refs[HALVES + h][...] = refs[h][:, h * width : (h + 1) * width]

    return call(body, "halve", tuple(pieces), [VMEM] * HALVES, [f32(rows, width)] * HALVES, [VMEM] * HALVES)


def columns(ref, h):
    width = ref.shape[1] // HALVES
    return ref.at[:, h * width : (h + 1) * width]


def base_rows(i, step, kkt, cost):
    rows, scen = kkt.shape[0], cost.shape[1]

    def body(kkt_ref, cost_ref, out_ref):
        out_ref[...] = jnp.dot(
            kkt_ref[i * step : (i + 1) * step, :], cost_ref[...], preferred_element_type=jnp.float32
        )

    return call(
        body,
        "base_rows",
        (kkt, cost),
        [VMEM, VMEM],
        f32(step, scen),
        VMEM,
        flops=2 * step * rows * scen,
        moved=3 << 20,
    )


def slots_of(table_ref, peers, blocks):
    out = []
    for r in range(peers):
        row = []
        for c in range(CAP):
            j = table_ref[CAP * r + c]
            b = table_ref[CAP * peers + CAP * r + c]
            read = jnp.maximum(j, 0)
            write = jnp.where(j < 0, blocks, j)
            row.append([pl.ds(pl.multiple_of(x * BLOCK, BLOCK), BLOCK) for x in (read, write, jnp.maximum(b, 0))] + [b])
        out.append(row)
    return out


def fold(x):
    return jnp.sum(x.reshape(-1, TILE, x.shape[-1]), axis=0)


def place(part_ref, totals, slots, owned):
    for o in range(owned):
        value = None
        for total, (_, _, _, b) in zip(totals, slots):
            mine = jnp.where(b == o, total, 0.0)
            value = mine if value is None else value + mine
        part_ref[o * BLOCK : (o + 1) * BLOCK, :] = value


def first_solve(h, table, pieces, dual, bases, kkt, owned, counting):
    peers = len(pieces)
    bound, scen = dual.shape
    width = scen // HALVES
    cols = slice(h * width, (h + 1) * width)
    own = owned * BLOCK
    sent = own + (TILE if counting else 0)
    step = bases[0].shape[0]
    chunks = bound // step

    def body(*refs):
        table_ref, refs = refs[0], refs[1:]
        piece, (dual_ref, kkt_ref), refs = refs[:peers], refs[peers : peers + 2], refs[peers + 2 :]
        piece = [ref if ref.shape[1] == width else columns(ref, h) for ref in piece]
        base_refs, z_ref, refs = refs[:chunks], refs[chunks], refs[chunks + 1 :]
        part, (drive_ref,) = refs[:peers], refs[peers:]
        slots = slots_of(table_ref, peers, bound // BLOCK)
        drive_ref[...] = jnp.zeros_like(drive_ref)
        for r in range(peers):
            for read, write, block, _ in slots[r]:
                drive_ref[write, :] = (penalty * (piece[r][block, :] - dual_ref[read, cols])).astype(jnp.bfloat16)
        for i in range(chunks):
            at = slice(i * step, (i + 1) * step)
            got = jnp.dot(kkt_ref[at, :bound], drive_ref[:bound, :], preferred_element_type=jnp.float32)
            z_ref[at, :] = (base_refs[i][:, cols] + got) + dual_ref[at, cols]
        for r in range(peers):
            place(part[r], [z_ref[read, :] for read, _, _, _ in slots[r]], slots[r], owned)
            if counting:
                row = lax.broadcasted_iota(jnp.int32, (TILE, width), 0)
                count = jnp.zeros((TILE, width), jnp.float32)
                for _, _, _, b in slots[r]:
                    count = count + jnp.where(row == b, 1.0, 0.0)
                part[r][own:, :] = count

    out = call(
        body,
        "first_solve",
        (table, *pieces, dual, kkt, *bases[:chunks]),
        [SMEM] + [VMEM] * (peers + 2 + chunks),
        [f32(bound, width)] + [f32(sent, width)] * peers,
        [VMEM] * (1 + peers),
        [pltpu.VMEM((bound + BLOCK, width), jnp.bfloat16)],
        flops=2 * bound * bound * width,
        moved=8 << 20,
    )
    return out[0], out[1:]


def second_solve(h, table, pieces, z, dual, bases, kkt, owned):
    peers = len(pieces)
    bound, scen = dual.shape
    step = bases[0].shape[0]
    chunks = bound // step
    width = scen // HALVES
    cols = slice(h * width, (h + 1) * width)
    own = owned * BLOCK

    def body(*refs):
        table_ref, refs = refs[0], refs[1:]
        piece, (z_ref, dual_ref, kkt_ref), refs = refs[:peers], refs[peers : peers + 3], refs[peers + 3 :]
        base_refs, refs = refs[:chunks], refs[chunks:]
        field_ref, drive_ref, next_ref, norm_ref, part = refs[0], refs[1], refs[2], refs[3], refs[4:]
        slots = slots_of(table_ref, peers, bound // BLOCK)
        drive_ref[...] = jnp.zeros_like(drive_ref)
        next_ref[:bound, :] = dual_ref[:, cols]
        gaps = jnp.zeros((TILE, width), jnp.float32)
        for r in range(peers):
            for read, write, block, b in slots[r]:
                fetched = piece[r][block, :]
                renewed_dual = z_ref[read, :] - fetched
                gap = renewed_dual - dual_ref[read, cols]
                gaps = gaps + jnp.where(b < 0, 0.0, fold(gap * gap))
                next_ref[write, :] = renewed_dual
                drive_ref[write, :] = (penalty * (fetched - renewed_dual)).astype(jnp.bfloat16)
        for i in range(chunks):
            at = slice(i * step, (i + 1) * step)
            got = jnp.dot(kkt_ref[at, :bound], drive_ref[:bound, :], preferred_element_type=jnp.float32)
            field_ref[at, :] = base_refs[i][:, cols] + got
        shifts = jnp.zeros((TILE, width), jnp.float32)
        for r in range(peers):
            totals = []
            for read, write, block, b in slots[r]:
                copies = field_ref[read, :]
                shift = copies - piece[r][block, :]
                shifts = shifts + jnp.where(b < 0, 0.0, fold(shift * shift))
                totals.append(copies + next_ref[read, :])
            for total, (_, write, _, _) in zip(totals, slots[r]):
                next_ref[write, :] = total
            place(part[r], totals, slots[r], owned)
        norm_ref[:TILE, :] = gaps
        norm_ref[TILE:, :] = shifts

    out = call(
        body,
        "second_solve",
        (table, *pieces, z, dual, kkt, *bases[:chunks]),
        [SMEM] + [VMEM] * (peers + 3 + chunks),
        [
            f32(bound, width),
            jax.ShapeDtypeStruct((bound + BLOCK, width), jnp.bfloat16),
            f32(bound + BLOCK, width),
            f32(2 * TILE, width),
        ]
        + [f32(own, width)] * peers,
        [VMEM] * (4 + peers),
        flops=2 * bound * bound * width,
        moved=8 << 20,
    )
    return out[0], out[1], out[2], out[3], out[4:]


def store_state(h, field, drive, bases, kkt, state):
    bound, width = field.shape
    rows = kkt.shape[0]
    step = bases[0].shape[0]
    cols = slice(h * width, (h + 1) * width)
    given = 0 if state is None else 1
    rest = bases[bound // step :]

    def body(field_ref, drive_ref, kkt_ref, *refs):
        base_refs, (state_hbm, rest_ref, sem) = refs[: len(rest)], refs[len(rest) + given :]
        loads = Loads(sem)
        loads.start("field", field_ref, state_hbm.at[:bound, cols])
        for i in range(len(rest)):
            at = slice(i * step, (i + 1) * step)
            there = slice(bound + i * step, bound + (i + 1) * step)
            got = jnp.dot(kkt_ref[there, :bound], drive_ref[:bound, :], preferred_element_type=jnp.float32)
            rest_ref[at, :] = base_refs[i][:, cols] + got
        loads.start("rest", rest_ref, state_hbm.at[bound:, cols])
        loads.wait("field")
        loads.wait("rest")

    before = () if state is None else (state,)
    return call(
        body,
        "store_state",
        (field, drive, kkt, *rest, *before),
        [VMEM] * (3 + len(rest)) + [HBM] * given,
        f32(rows, HALVES * width),
        HBM,
        [pltpu.VMEM((rows - bound, width), jnp.float32), pltpu.SemaphoreType.DMA((2,))],
        aliases={3 + len(rest): 0} if given else None,
        flops=2 * bound * (rows - bound) * width,
        moved=4 << 20,
    )


def add_pairs(pairs):
    def body(*refs):
        for i in range(len(pairs)):
            refs[2 * len(pairs) + i][...] = refs[2 * i][...] + refs[2 * i + 1][...]

    out = call(
        body,
        "add_pairs",
        tuple(x for pair in pairs for x in pair),
        [VMEM] * (2 * len(pairs)),
        [f32(*pair[0].shape) for pair in pairs],
        [VMEM] * len(pairs),
    )
    return list(out)


def renew(h, parts, before, count, norms):
    own, width = before.shape[0], parts[0].shape[1]
    owned = own // BLOCK
    counted = count is None

    def body(*refs):
        parts_ref, refs = refs[: len(parts)], refs[len(parts) :]
        before_ref, refs = refs[0] if before.shape[1] == width else columns(refs[0], h), refs[1:]
        if not counted:
            count_ref, refs = refs[0], refs[1:]
        norm_refs, refs = refs[: len(norms)], refs[len(norms) :]
        new_ref, moved_ref = refs[0], refs[1]

        def total(at):
            value = parts_ref[0][at, :]
            for ref in parts_ref[1:]:
                value = value + ref[at, :]
            return value

        if counted:
            tile = total(slice(own, own + TILE))
            refs[2][...] = tile
        else:
            tile = count_ref[...]
        moved = jnp.zeros((TILE, width), jnp.float32)
        for b in range(owned):
            at = slice(b * BLOCK, (b + 1) * BLOCK)
            many = tile[b : b + 1, :]
            value = total(at) / jnp.maximum(many, 1.0)
            change = value - before_ref[at, :]
            moved = moved + many * fold(change * change)
            new_ref[at, :] = value
        moved_ref[...] = moved
        if norms:
            gaps = norm_refs[0][...] + norm_refs[3][...]
            sums = [
                gaps[:TILE, :],
                norm_refs[1][...] + norm_refs[4][...],
                gaps[TILE:, :],
                norm_refs[2][...] + moved,
            ]
            row = lax.broadcasted_iota(jnp.int32, (TILE, width), 0)
            block = jnp.zeros((TILE, width), jnp.float32)
            for i, x in enumerate(sums):
                block = jnp.where(row == i, jnp.sum(x, axis=0, keepdims=True), block)
            new_ref[own:, :] = block

    ins = (*parts, before) + (() if counted else (count,)) + tuple(norms)
    outs = [f32(own + (TILE if norms else 0), width), f32(TILE, width)] + ([f32(TILE, width)] if counted else [])
    return call(body, "renew", ins, [VMEM] * len(ins), outs, [VMEM] * len(outs))


def finish(h, table, pieces, z, scen, owned, outputs):
    peers = len(pieces)
    bound, width = z.shape[0] - BLOCK, z.shape[1]
    cols = slice(h * width, (h + 1) * width)
    own = owned * BLOCK
    given = len(outputs)

    def body(*refs):
        table_ref, refs = refs[0], refs[1:]
        piece, z_ref, refs = refs[:peers], refs[peers], refs[peers + 1 + given :]
        dual_hbm, cons_hbm, dual_ref, sem = refs
        loads = Loads(sem)
        loads.start("cons", piece[0].at[:own, :], cons_hbm.at[:, cols])
        dual_ref[:bound, :] = z_ref[:bound, :]
        for r, slots in enumerate(slots_of(table_ref, peers, bound // BLOCK)):
            for read, write, block, _ in slots:
                dual_ref[write, :] = z_ref[read, :] - piece[r][block, :]
        loads.start("dual", dual_ref.at[:bound, :], dual_hbm.at[:, cols])
        loads.wait("dual")
        loads.wait("cons")

    return call(
        body,
        "finish",
        (table, *pieces, z, *outputs),
        [SMEM] + [VMEM] * (peers + 1) + [HBM] * given,
        [f32(bound, scen), f32(own, scen)],
        [HBM] * 2,
        [pltpu.VMEM((bound + BLOCK, width), jnp.float32), pltpu.SemaphoreType.DMA((2,))],
        aliases={peers + 2: 0, peers + 3: 1} if given else None,
        moved=3 << 20,
    )


def sum_tails(pieces, own, done):
    peers, width = len(pieces), pieces[0].shape[1]

    def body(*refs):
        total = refs[0][own:, :]
        for ref in refs[1:peers]:
            total = total + ref[own:, :]
        refs[-1][...] = total

    ins = (*pieces, *done)
    return call(body, "sum_tails", ins, [VMEM] * peers + [HBM] * len(done), f32(TILE, width), VMEM)


def norm_table(tiles, scale):
    def body(*refs):
        total = refs[0][...]
        for ref in refs[1:-1]:
            total = total + ref[...]
        total = jnp.sum(total, axis=1, keepdims=True)
        row = lax.broadcasted_iota(jnp.int32, (ITERS, 2), 0)
        col = lax.broadcasted_iota(jnp.int32, (ITERS, 2), 1)
        primal = jnp.where(row == 0, total[0:1, :], total[2:3, :] - total[3:4, :])
        moved = penalty * penalty * jnp.where(row == 0, total[1:2, :], total[3:4, :])
        refs[-1][...] = jnp.sqrt(jnp.maximum(jnp.where(col == 0, primal, moved), 0.0) / scale)

    return call(body, "norm_table", tuple(tiles), [VMEM] * len(tiles), f32(ITERS, 2), VMEM)


def shards(kkt, cost, dual, cons, target):
    scen = cost.shape[1]
    owned = cons.shape[0] // BLOCK
    peers = lax.axis_size("region")
    subs = lax.axis_size("sub")
    order = sorted(range(peers), key=lambda region: ring_place(region, peers))
    ahead = [(order[i], order[(i + 1) % peers]) for i in range(peers)]
    behind = [(b, a) for a, b in ahead]

    def forward(x):
        return lax.ppermute(x, "region", ahead)

    def backward(x):
        return lax.ppermute(x, "region", behind)

    def reach(h):
        long, short = peers // 2, (peers - 1) // 2
        return (long, short) if h % 2 == 0 else (short, long)

    def gather(h, piece, beside=lambda k, x: x):
        far, near = reach(h)
        pieces = [piece] * peers
        f = b = piece
        for k in range(1, max(far, near) + 1):
            values = yield ([f] if k <= far else []) + ([b] if k <= near else [])
            values = beside(k, values)
            if k <= far:
                f = pieces[(peers - k) % peers] = forward(values.pop(0))
            if k <= near:
                b = pieces[k] = backward(values.pop(0))
        return pieces

    def scatter(h, parts):
        far, near = reach(h)
        f, b = parts[far], parts[peers - near]
        for k in range(1, max(far, near) + 1):
            going, coming = f, b
            values = yield ([f] if k <= far else []) + ([b] if k <= near else [])
            f = forward(values.pop(0)) if k <= far else going
            b = backward(values.pop(0)) if k <= near else coming
            pairs = []
            if k < far:
                pairs.append((f, parts[far - k]))
            if k < near:
                pairs.append((b, parts[peers - near + k]))
            if pairs:
                added = [add_pairs([pair])[0] for pair in pairs]
                if k < far:
                    f = added.pop(0)
                if k < near:
                    b = added.pop(0)
        return [parts[0], f, b]

    region = lax.axis_index("region").astype(jnp.int32).reshape(1)
    halves = split(cons)
    table, (kkt, cost, dual) = prepare(region, target, owned, kkt, cost, dual, peers)
    step = math.gcd(dual.shape[0], kkt.shape[0])
    chunks = kkt.shape[0] // step
    bases = []

    def beside(h, k, values):
        turn = HALVES * (k - 1) + h
        some = [dual] if turn == LOAD_TURN else []
        while len(bases) < min(chunks, BASE_AT.get(turn, 0)):
            bases.append(base_rows(len(bases), step, kkt, cost))
            some.append(bases[-1])
        return tie(values, [], some) if some else values

    known = {"state": None, "outputs": (), "count": None, "norms": []}

    def half(h):
        last = h == HALVES - 1
        pieces = yield from gather(h, halves[h], lambda k, values: beside(h, k, values))
        z, parts = first_solve(h, table, pieces, dual, bases, kkt, owned, h == 0)
        arrived = yield from scatter(h, parts)
        out = renew(h, arrived, halves[h], known["count"], ())
        averages, moved = out[0], out[1]
        if known["count"] is None:
            known["count"] = out[2]
        pieces = yield from gather(h, averages)
        field, drive, z, gaps, parts = second_solve(h, table, pieces, z, dual, bases, kkt, owned)
        known["state"] = store_state(h, field, drive, bases, kkt, known["state"])
        arrived = yield from scatter(h, parts)
        norms = known["norms"] + [gaps, moved]
        out = renew(h, arrived, averages, known["count"], norms if last else ())
        known["norms"] = norms + [out[1]]
        pieces = yield from gather(h, out[0])
        if last:
            known["tail"] = sum_tails(pieces, owned * BLOCK, [*known["outputs"], known["state"]])
        known["outputs"] = finish(h, table, pieces, z, scen, owned, known["outputs"])

    turns = [half(h) for h in range(HALVES)]
    waiting = [next(turn) for turn in turns]
    which = LEAD * [0]
    while any(w is not None for w in waiting):
        h = which.pop(0) if which else next_turn(waiting, h)
        values = list(waiting[h])
        try:
            waiting[h] = turns[h].send(values)
        except StopIteration:
            waiting[h] = None
    tail = known["tail"]
    turned = [lax.ppermute(tail, "sub", [(i, (i + k) % subs) for i in range(subs)]) for k in range(1, subs)]
    norms = norm_table([tail, *turned], float(peers * subs * scen * BLOCK))
    return (known["state"], *known["outputs"], norms)


def next_turn(waiting, h):
    for k in range(1, len(waiting) + 1):
        if waiting[(h + k) % len(waiting)] is not None:
            return (h + k) % len(waiting)


def solution(mesh):
    spec = P(("region", "sub"), None)
    return jax.shard_map(
        shards, mesh=mesh, in_specs=(spec,) * 5, out_specs=(spec, spec, spec, P()), check_vma=False
    )
```

```python
import math

import jax
import jax.numpy as jnp
from jax import lax
from jax.experimental import pallas as pl
from jax.experimental.pallas import tpu as pltpu
from jax.sharding import PartitionSpec as P

BLOCK = 128
CAP = 2
ITERS = 2
HALVES = 2
TILE = 8
LEAD = 1
LOAD_TURN = 2
BASE_AT = {4: 2, 6: 4}
CUTS = 8


penalty = 1.5

VMEM = pl.BlockSpec(memory_space=pltpu.VMEM)
SMEM = pl.BlockSpec(memory_space=pltpu.SMEM)
HBM = pl.BlockSpec(memory_space=pltpu.HBM)


def grid_of(peers):
    columns = 1
    while (2 * columns) ** 2 <= peers:
        columns *= 2
    return peers // columns, columns


def ring_place(region, peers):
    rows, columns = grid_of(peers)
    row, column = region // columns, region % columns
    up = rows - 1 - row
    if columns == 1:
        return row
    right = up % 2 == 0
    if isinstance(region, int):
        if column == 0:
            return row
        return rows + up * (columns - 1) + (column - 1 if right else columns - 1 - column)
    along = jnp.where(right, column - 1, columns - 1 - column)
    return jnp.where(column == 0, row, rows + up * (columns - 1) + along)


def f32(*shape):
    return jax.ShapeDtypeStruct(shape, jnp.float32)


def call(body, name, ins, in_specs, outs, out_specs, scratch=(), aliases=None, flops=0, moved=1 << 20, room=4, pins=()):
    ins = tuple(pltpu.with_memory_space_constraint(x, pltpu.HBM) if spec is HBM else x for x, spec in zip(ins, in_specs))
    many = isinstance(outs, (list, tuple))
    shapes, specs = (list(outs), list(out_specs)) if many else ([outs], [out_specs])
    for i, spec in enumerate(specs):
        if spec is HBM:
            shapes[i] = pltpu.HBM(shapes[i].shape, shapes[i].dtype)
        elif i in pins:
            shapes[i] = pltpu.VMEM(shapes[i].shape, shapes[i].dtype)
    return pl.pallas_call(
        body,
        name=name,
        out_shape=shapes if many else shapes[0],
        in_specs=in_specs,
        out_specs=out_specs,
        scratch_shapes=scratch,
        input_output_aliases=aliases or {},
        cost_estimate=pl.CostEstimate(flops=flops, bytes_accessed=moved, transcendentals=0),
        compiler_params=pltpu.CompilerParams(vmem_limit_bytes=room << 20),
    )(*ins)


def tie(values, others, near=()):
    values, others = list(values), list(others)

    def body(*refs):
        del refs

    out = call(
        body,
        "tie",
        (*values, *others, *near),
        [VMEM] * len(values) + [HBM] * len(others) + [VMEM] * len(near),
        [f32(*x.shape) for x in values],
        [VMEM] * len(values),
        aliases={i: i for i in range(len(values))},
        moved=0,
    )
    return list(out)


class Loads:
    def __init__(self, sem):
        self.sem, self.used, self.flying = sem, 0, {}

    def start(self, name, src, dst):
        copy = pltpu.make_async_copy(src, dst, self.sem.at[self.used])
        copy.start()
        self.used += 1
        self.flying[name] = copy

    def wait(self, name):
        self.flying.pop(name).wait()


def split(cons):
    rows, scen = cons.shape
    width = scen // HALVES

    def body(cons_ref, *refs):
        copies = [
            pltpu.make_async_copy(cons_ref.at[:, h * width : (h + 1) * width], refs[h], refs[-1].at[h])
            for h in range(HALVES)
        ]
        for copy in copies:
            copy.start()
        for copy in copies:
            copy.wait()

    return call(
        body, "split", (cons,), [HBM], [f32(rows, width)] * HALVES, [VMEM] * HALVES, [pltpu.SemaphoreType.DMA((HALVES,))]
    )


def prepare(region, target, owned, kkt, cost, dual, peers):
    blocks = target.shape[1]
    arrays = (kkt, cost, dual)
    cuts = (CUTS, 1, 1)

    def body(region_ref, target_hbm, *refs):
        from_refs, table_ref, to_refs, target_ref, sem = refs[:3], refs[3], refs[4:7], refs[7], refs[8]
        loads = Loads(sem)
        loads.start("target", target_hbm, target_ref)
        for i, (src, dst) in enumerate(zip(from_refs, to_refs)):
            size = src.shape[0] // cuts[i]
            for c in range(cuts[i]):
                at = slice(c * size, (c + 1) * size)
                loads.start((i, c), src.at[at, :], dst.at[at, :])
        here = ring_place(region_ref[0], peers)
        for i in range(2 * CAP * peers):
            table_ref[i] = -1
        loads.wait("target")
        for j in range(blocks):
            t = target_ref[0, j]

            @pl.when(t >= 0)
            def _(t=t, j=j):
                owner = t // owned
                ahead = ring_place(owner, peers) - here
                ahead = jnp.where(ahead < 0, ahead + peers, ahead)
                first = CAP * ahead
                at = first + jnp.where(table_ref[first] >= 0, 1, 0)
                table_ref[at] = j
                table_ref[CAP * peers + at] = t - owner * owned

        for i in range(3):
            for c in range(cuts[i]):
                loads.wait((i, c))

    out = call(
        body,
        "prepare",
        (region, target, *arrays),
        [SMEM] + [HBM] * 4,
        [jax.ShapeDtypeStruct((2 * CAP * peers,), jnp.int32)] + [jax.ShapeDtypeStruct(x.shape, x.dtype) for x in arrays],
        [SMEM] + [VMEM] * 3,
        [pltpu.SMEM(target.shape, jnp.int32), pltpu.SemaphoreType.DMA((1 + sum(cuts),))],
        moved=12 << 20,
    )
    return out[0], out[1:]


def halve(pieces):
    rows, scen = pieces[0].shape
    width = scen // HALVES

    def body(*refs):
        for h in range(HALVES):
            refs[HALVES + h][...] = refs[h][:, h * width : (h + 1) * width]

    return call(body, "halve", tuple(pieces), [VMEM] * HALVES, [f32(rows, width)] * HALVES, [VMEM] * HALVES)


def columns(ref, h):
    width = ref.shape[1] // HALVES
    return ref.at[:, h * width : (h + 1) * width]


def base_rows(i, step, kkt, cost):
    rows, scen = kkt.shape[0], cost.shape[1]

    def body(kkt_ref, cost_ref, out_ref):
        out_ref[...] = jnp.dot(
            kkt_ref[i * step : (i + 1) * step, :], cost_ref[...], preferred_element_type=jnp.float32
        )

    return call(
        body,
        "base_rows",
        (kkt, cost),
        [VMEM, VMEM],
        f32(step, scen),
        VMEM,
        flops=2 * step * rows * scen,
        moved=3 << 20,
    )


def slots_of(table_ref, peers, blocks):
    out = []
    for r in range(peers):
        row = []
        for c in range(CAP):
            j = table_ref[CAP * r + c]
            b = table_ref[CAP * peers + CAP * r + c]
            read = jnp.maximum(j, 0)
            write = jnp.where(j < 0, blocks, j)
            row.append([pl.ds(pl.multiple_of(x * BLOCK, BLOCK), BLOCK) for x in (read, write, jnp.maximum(b, 0))] + [b])
        out.append(row)
    return out


def fold(x):
    return jnp.sum(x.reshape(-1, TILE, x.shape[-1]), axis=0)


def place(part_ref, totals, slots, owned):
    for o in range(owned):
        value = None
        for total, (_, _, _, b) in zip(totals, slots):
            mine = jnp.where(b == o, total, 0.0)
            value = mine if value is None else value + mine
        part_ref[o * BLOCK : (o + 1) * BLOCK, :] = value


def first_solve(h, table, pieces, dual, bases, kkt, owned, counting):
    peers = len(pieces)
    bound, scen = dual.shape
    width = scen // HALVES
    cols = slice(h * width, (h + 1) * width)
    own = owned * BLOCK
    sent = own + (TILE if counting else 0)
    step = bases[0].shape[0]
    chunks = bound // step

    def body(*refs):
        table_ref, refs = refs[0], refs[1:]
        piece, (dual_ref, kkt_ref), refs = refs[:peers], refs[peers : peers + 2], refs[peers + 2 :]
        piece = [ref if ref.shape[1] == width else columns(ref, h) for ref in piece]
        base_refs, z_ref, refs = refs[:chunks], refs[chunks], refs[chunks + 1 :]
        part, (drive_ref,) = refs[:peers], refs[peers:]
        slots = slots_of(table_ref, peers, bound // BLOCK)
        drive_ref[...] = jnp.zeros_like(drive_ref)
        for r in range(peers):
            for read, write, block, _ in slots[r]:
                drive_ref[write, :] = (penalty * (piece[r][block, :] - dual_ref[read, cols])).astype(jnp.bfloat16)
        for i in range(chunks):
            at = slice(i * step, (i + 1) * step)
            got = jnp.dot(kkt_ref[at, :bound], drive_ref[:bound, :], preferred_element_type=jnp.float32)
            z_ref[at, :] = (base_refs[i][:, cols] + got) + dual_ref[at, cols]
        for r in range(peers):
            place(part[r], [z_ref[read, :] for read, _, _, _ in slots[r]], slots[r], owned)
            if counting:
                row = lax.broadcasted_iota(jnp.int32, (TILE, width), 0)
                count = jnp.zeros((TILE, width), jnp.float32)
                for _, _, _, b in slots[r]:
                    count = count + jnp.where(row == b, 1.0, 0.0)
                part[r][own:, :] = count

    out = call(
        body,
        "first_solve",
        (table, *pieces, dual, kkt, *bases[:chunks]),
        [SMEM] + [VMEM] * (peers + 2 + chunks),
        [f32(bound, width)] + [f32(sent, width)] * peers,
        [VMEM] * (1 + peers),
        [pltpu.VMEM((bound + BLOCK, width), jnp.bfloat16)],
        flops=2 * bound * bound * width,
        moved=8 << 20,
    )
    return out[0], out[1:]


def second_solve(h, table, pieces, z, dual, bases, kkt, owned):
    peers = len(pieces)
    bound, scen = dual.shape
    step = bases[0].shape[0]
    chunks = bound // step
    width = scen // HALVES
    cols = slice(h * width, (h + 1) * width)
    own = owned * BLOCK

    def body(*refs):
        table_ref, refs = refs[0], refs[1:]
        piece, (z_ref, dual_ref, kkt_ref), refs = refs[:peers], refs[peers : peers + 3], refs[peers + 3 :]
        base_refs, refs = refs[:chunks], refs[chunks:]
        field_ref, drive_ref, next_ref, norm_ref, part = refs[0], refs[1], refs[2], refs[3], refs[4:]
        slots = slots_of(table_ref, peers, bound // BLOCK)
        drive_ref[...] = jnp.zeros_like(drive_ref)
        next_ref[:bound, :] = dual_ref[:, cols]
        gaps = jnp.zeros((TILE, width), jnp.float32)
        for r in range(peers):
            for read, write, block, b in slots[r]:
                fetched = piece[r][block, :]
                renewed_dual = z_ref[read, :] - fetched
                gap = renewed_dual - dual_ref[read, cols]
                gaps = gaps + jnp.where(b < 0, 0.0, fold(gap * gap))
                next_ref[write, :] = renewed_dual
                drive_ref[write, :] = (penalty * (fetched - renewed_dual)).astype(jnp.bfloat16)
        for i in range(chunks):
            at = slice(i * step, (i + 1) * step)
            got = jnp.dot(kkt_ref[at, :bound], drive_ref[:bound, :], preferred_element_type=jnp.float32)
            field_ref[at, :] = base_refs[i][:, cols] + got
        shifts = jnp.zeros((TILE, width), jnp.float32)
        for r in range(peers):
            totals = []
            for read, write, block, b in slots[r]:
                copies = field_ref[read, :]
                shift = copies - piece[r][block, :]
                shifts = shifts + jnp.where(b < 0, 0.0, fold(shift * shift))
                totals.append(copies + next_ref[read, :])
            for total, (_, write, _, _) in zip(totals, slots[r]):
                next_ref[write, :] = total
            place(part[r], totals, slots[r], owned)
        norm_ref[:TILE, :] = gaps
        norm_ref[TILE:, :] = shifts

    out = call(
        body,
        "second_solve",
        (table, *pieces, z, dual, kkt, *bases[:chunks]),
        [SMEM] + [VMEM] * (peers + 3 + chunks),
        [
            f32(bound, width),
            jax.ShapeDtypeStruct((bound + BLOCK, width), jnp.bfloat16),
            f32(bound + BLOCK, width),
            f32(2 * TILE, width),
        ]
        + [f32(own, width)] * peers,
        [VMEM] * (4 + peers),
        flops=2 * bound * bound * width,
        moved=8 << 20,
    )
    return out[0], out[1], out[2], out[3], out[4:]


def store_state(fields, drives, bases, kkt):
    bound, width = fields[0].shape
    rows = kkt.shape[0]
    step = bases[0].shape[0]
    rest = bases[bound // step :]

    def body(*refs):
        field_refs, drive_refs, kkt_ref, refs = refs[:HALVES], refs[HALVES : 2 * HALVES], refs[2 * HALVES], refs[2 * HALVES + 1 :]
        base_refs, (state_hbm, rest_ref, sem) = refs[: len(rest)], refs[len(rest) :]
        loads = Loads(sem)
        for h in range(HALVES):
            cols = slice(h * width, (h + 1) * width)
            loads.start(h, field_refs[h], state_hbm.at[:bound, cols])
        for h in range(HALVES):
            cols = slice(h * width, (h + 1) * width)
            for i in range(len(rest)):
                at = slice(i * step, (i + 1) * step)
                there = slice(bound + i * step, bound + (i + 1) * step)
                got = jnp.dot(kkt_ref[there, :bound], drive_refs[h][:bound, :], preferred_element_type=jnp.float32)
                rest_ref[at, cols] = base_refs[i][:, cols] + got
        loads.start("rest", rest_ref, state_hbm.at[bound:, :])
        for h in range(HALVES):
            loads.wait(h)
        loads.wait("rest")

    return call(
        body,
        "store_state",
        (*fields, *drives, kkt, *rest),
        [VMEM] * (2 * HALVES + 1 + len(rest)),
        f32(rows, HALVES * width),
        HBM,
        [pltpu.VMEM((rows - bound, HALVES * width), jnp.float32), pltpu.SemaphoreType.DMA((HALVES + 1,))],
        flops=2 * bound * (rows - bound) * HALVES * width,
        moved=4 << 20,
    )


def add_pairs(pairs):
    def body(*refs):
        for i in range(len(pairs)):
            refs[2 * len(pairs) + i][...] = refs[2 * i][...] + refs[2 * i + 1][...]

    out = call(
        body,
        "add_pairs",
        tuple(x for pair in pairs for x in pair),
        [VMEM] * (2 * len(pairs)),
        [f32(*pair[0].shape) for pair in pairs],
        [VMEM] * len(pairs),
    )
    return list(out)


def renew(h, parts, before, count, norms):
    own, width = before.shape[0], parts[0].shape[1]
    owned = own // BLOCK
    counted = count is None

    def body(*refs):
        parts_ref, refs = refs[: len(parts)], refs[len(parts) :]
        before_ref, refs = refs[0] if before.shape[1] == width else columns(refs[0], h), refs[1:]
        if not counted:
            count_ref, refs = refs[0], refs[1:]
        norm_refs, refs = refs[: len(norms)], refs[len(norms) :]
        new_ref, moved_ref = refs[0], refs[1]

        def total(at):
            value = parts_ref[0][at, :]
            for ref in parts_ref[1:]:
                value = value + ref[at, :]
            return value

        if counted:
            tile = total(slice(own, own + TILE))
            refs[2][...] = tile
        else:
            tile = count_ref[...]
        moved = jnp.zeros((TILE, width), jnp.float32)
        for b in range(owned):
            at = slice(b * BLOCK, (b + 1) * BLOCK)
            many = tile[b : b + 1, :]
            value = total(at) / jnp.maximum(many, 1.0)
            change = value - before_ref[at, :]
            moved = moved + many * fold(change * change)
            new_ref[at, :] = value
        moved_ref[...] = moved
        if norms:
            gaps = norm_refs[0][...] + norm_refs[3][...]
            sums = [
                gaps[:TILE, :],
                norm_refs[1][...] + norm_refs[4][...],
                gaps[TILE:, :],
                norm_refs[2][...] + moved,
            ]
            row = lax.broadcasted_iota(jnp.int32, (TILE, width), 0)
            block = jnp.zeros((TILE, width), jnp.float32)
            for i, x in enumerate(sums):
                block = jnp.where(row == i, jnp.sum(x, axis=0, keepdims=True), block)
            new_ref[own:, :] = block

    ins = (*parts, before) + (() if counted else (count,)) + tuple(norms)
    outs = [f32(own + (TILE if norms else 0), width), f32(TILE, width)] + ([f32(TILE, width)] if counted else [])
    return call(body, "renew", ins, [VMEM] * len(ins), outs, [VMEM] * len(outs))


def finish(table, pieces, zs, owned):
    peers = len(pieces[0])
    bound, width = zs[0].shape[0] - BLOCK, zs[0].shape[1]
    own = owned * BLOCK

    def body(*refs):
        table_ref, refs = refs[0], refs[1:]
        halves, refs = [refs[h * peers : (h + 1) * peers] for h in range(HALVES)], refs[HALVES * peers :]
        z_refs, (dual_hbm, cons_hbm, dual_ref, sem) = refs[:HALVES], refs[HALVES:]
        loads = Loads(sem)
        slots = slots_of(table_ref, peers, bound // BLOCK)
        for h in range(HALVES):
            cols = slice(h * width, (h + 1) * width)
            loads.start(("cons", h), halves[h][0].at[:own, :], cons_hbm.at[:, cols])
            dual_ref[:bound, cols] = z_refs[h][:bound, :]
            for r in range(peers):
                for read, write, block, _ in slots[r]:
                    dual_ref[write, cols] = z_refs[h][read, :] - halves[h][r][block, :]
        loads.start("dual", dual_ref.at[:bound, :], dual_hbm)
        for name in list(loads.flying):
            loads.wait(name)

    scen = HALVES * width
    return call(
        body,
        "finish",
        (table, *[piece for half in pieces for piece in half], *zs),
        [SMEM] + [VMEM] * (HALVES * (peers + 1)),
        [f32(bound, scen), f32(own, scen)],
        [HBM] * 2,
        [pltpu.VMEM((bound + BLOCK, scen), jnp.float32), pltpu.SemaphoreType.DMA((1 + HALVES,))],
        moved=3 << 20,
        room=14,
    )


def sum_tails(pieces, own, done):
    peers, width = len(pieces), pieces[0].shape[1]

    def body(*refs):
        total = refs[0][own:, :]
        for ref in refs[1:peers]:
            total = total + ref[own:, :]
        refs[-1][...] = total

    ins = (*pieces, *done)
    return call(body, "sum_tails", ins, [VMEM] * peers + [HBM] * len(done), f32(TILE, width), VMEM)


def norm_table(tiles, scale):
    def body(*refs):
        total = refs[0][...]
        for ref in refs[1:-1]:
            total = total + ref[...]
        total = jnp.sum(total, axis=1, keepdims=True)
        row = lax.broadcasted_iota(jnp.int32, (ITERS, 2), 0)
        col = lax.broadcasted_iota(jnp.int32, (ITERS, 2), 1)
        primal = jnp.where(row == 0, total[0:1, :], total[2:3, :] - total[3:4, :])
        moved = penalty * penalty * jnp.where(row == 0, total[1:2, :], total[3:4, :])
        refs[-1][...] = jnp.sqrt(jnp.maximum(jnp.where(col == 0, primal, moved), 0.0) / scale)

    return call(body, "norm_table", tuple(tiles), [VMEM] * len(tiles), f32(ITERS, 2), VMEM)


def shards(kkt, cost, dual, cons, target):
    scen = cost.shape[1]
    owned = cons.shape[0] // BLOCK
    peers = lax.axis_size("region")
    subs = lax.axis_size("sub")
    order = sorted(range(peers), key=lambda region: ring_place(region, peers))
    ahead = [(order[i], order[(i + 1) % peers]) for i in range(peers)]
    behind = [(b, a) for a, b in ahead]

    def forward(x):
        return lax.ppermute(x, "region", ahead)

    def backward(x):
        return lax.ppermute(x, "region", behind)

    def reach(h):
        long, short = peers // 2, (peers - 1) // 2
        return (long, short) if h % 2 == 0 else (short, long)

    def gather(h, piece, beside=lambda k, x: x):
        far, near = reach(h)
        pieces = [piece] * peers
        f = b = piece
        for k in range(1, max(far, near) + 1):
            values = yield ([f] if k <= far else []) + ([b] if k <= near else [])
            values = beside(k, values)
            if k <= far:
                f = pieces[(peers - k) % peers] = forward(values.pop(0))
            if k <= near:
                b = pieces[k] = backward(values.pop(0))
        return pieces

    def scatter(h, parts):
        far, near = reach(h)
        f, b = parts[far], parts[peers - near]
        for k in range(1, max(far, near) + 1):
            going, coming = f, b
            values = yield ([f] if k <= far else []) + ([b] if k <= near else [])
            f = forward(values.pop(0)) if k <= far else going
            b = backward(values.pop(0)) if k <= near else coming
            pairs = []
            if k < far:
                pairs.append((f, parts[far - k]))
            if k < near:
                pairs.append((b, parts[peers - near + k]))
            if pairs:
                added = [add_pairs([pair])[0] for pair in pairs]
                if k < far:
                    f = added.pop(0)
                if k < near:
                    b = added.pop(0)
        return [parts[0], f, b]

    region = lax.axis_index("region").astype(jnp.int32).reshape(1)
    halves = split(cons)
    table, (kkt, cost, dual) = prepare(region, target, owned, kkt, cost, dual, peers)
    step = math.gcd(dual.shape[0], kkt.shape[0])
    chunks = kkt.shape[0] // step
    bases = []

    def beside(h, k, values):
        turn = HALVES * (k - 1) + h
        some = [dual] if turn == LOAD_TURN else []
        while len(bases) < min(chunks, BASE_AT.get(turn, 0)):
            bases.append(base_rows(len(bases), step, kkt, cost))
            some.append(bases[-1])
        return tie(values, [], some) if some else values

    known = {"count": None, "norms": [], "solved": [], "last": []}

    def half(h):
        last = h == HALVES - 1
        pieces = yield from gather(h, halves[h], lambda k, values: beside(h, k, values))
        z, parts = first_solve(h, table, pieces, dual, bases, kkt, owned, h == 0)
        arrived = yield from scatter(h, parts)
        out = renew(h, arrived, halves[h], known["count"], ())
        averages, moved = out[0], out[1]
        if known["count"] is None:
            known["count"] = out[2]
        pieces = yield from gather(h, averages)
        field, drive, z, gaps, parts = second_solve(h, table, pieces, z, dual, bases, kkt, owned)
        known["solved"].append((field, drive))
        arrived = yield from scatter(h, parts)
        norms = known["norms"] + [gaps, moved]
        out = renew(h, arrived, averages, known["count"], norms if last else ())
        known["norms"] = norms + [out[1]]
        pieces = yield from gather(h, out[0])
        known["last"].append((pieces, z))

    turns = [half(h) for h in range(HALVES)]
    waiting = [next(turn) for turn in turns]
    which = LEAD * [0]
    while any(w is not None for w in waiting):
        h = which.pop(0) if which else next_turn(waiting, h)
        values = list(waiting[h])
        try:
            waiting[h] = turns[h].send(values)
        except StopIteration:
            waiting[h] = None
    fields, drives = zip(*known["solved"])
    state = store_state(fields, drives, bases, kkt)
    pieces, zs = zip(*known["last"])
    tail = sum_tails(pieces[-1], owned * BLOCK, [state])
    turned = [lax.ppermute(tail, "sub", [(i, (i + k) % subs) for i in range(subs)]) for k in range(1, subs)]
    norms = norm_table([tail, *turned], float(peers * subs * scen * BLOCK))
    return (state, *finish(table, pieces, zs, owned), norms)


def next_turn(waiting, h):
    for k in range(1, len(waiting) + 1):
        if waiting[(h + k) % len(waiting)] is not None:
            return (h + k) % len(waiting)


def solution(mesh):
    spec = P(("region", "sub"), None)
    return jax.shard_map(
        shards, mesh=mesh, in_specs=(spec,) * 5, out_specs=(spec, spec, spec, P()), check_vma=False
    )
```

```python
import math

import jax
import jax.numpy as jnp
from jax import lax
from jax.experimental import pallas as pl
from jax.experimental.pallas import tpu as pltpu
from jax.sharding import PartitionSpec as P

BLOCK = 128
CAP = 2
ITERS = 2
HALVES = 2
TILE = 8
LEAD = 1
LOAD_TURN = 2
BASE_AT = {4: 2, 6: 4}
CUTS = 8


penalty = 1.5

VMEM = pl.BlockSpec(memory_space=pltpu.VMEM)
SMEM = pl.BlockSpec(memory_space=pltpu.SMEM)
HBM = pl.BlockSpec(memory_space=pltpu.HBM)


def grid_of(peers):
    columns = 1
    while (2 * columns) ** 2 <= peers:
        columns *= 2
    return peers // columns, columns


def ring_place(region, peers):
    rows, columns = grid_of(peers)
    row, column = region // columns, region % columns
    up = rows - 1 - row
    if columns == 1:
        return row
    right = up % 2 == 0
    if isinstance(region, int):
        if column == 0:
            return row
        return rows + up * (columns - 1) + (column - 1 if right else columns - 1 - column)
    along = jnp.where(right, column - 1, columns - 1 - column)
    return jnp.where(column == 0, row, rows + up * (columns - 1) + along)


def f32(*shape):
    return jax.ShapeDtypeStruct(shape, jnp.float32)


def call(body, name, ins, in_specs, outs, out_specs, scratch=(), aliases=None, flops=0, moved=1 << 20, room=4, pins=()):
    ins = tuple(pltpu.with_memory_space_constraint(x, pltpu.HBM) if spec is HBM else x for x, spec in zip(ins, in_specs))
    many = isinstance(outs, (list, tuple))
    shapes, specs = (list(outs), list(out_specs)) if many else ([outs], [out_specs])
    for i, spec in enumerate(specs):
        if spec is HBM:
            shapes[i] = pltpu.HBM(shapes[i].shape, shapes[i].dtype)
        elif i in pins:
            shapes[i] = pltpu.VMEM(shapes[i].shape, shapes[i].dtype)
    return pl.pallas_call(
        body,
        name=name,
        out_shape=shapes if many else shapes[0],
        in_specs=in_specs,
        out_specs=out_specs,
        scratch_shapes=scratch,
        input_output_aliases=aliases or {},
        cost_estimate=pl.CostEstimate(flops=flops, bytes_accessed=moved, transcendentals=0),
        compiler_params=pltpu.CompilerParams(vmem_limit_bytes=room << 20),
    )(*ins)


def tie(values, others, near=()):
    values, others = list(values), list(others)

    def body(*refs):
        del refs

    out = call(
        body,
        "tie",
        (*values, *others, *near),
        [VMEM] * len(values) + [HBM] * len(others) + [VMEM] * len(near),
        [f32(*x.shape) for x in values],
        [VMEM] * len(values),
        aliases={i: i for i in range(len(values))},
        moved=0,
    )
    return list(out)


class Loads:
    def __init__(self, sem):
        self.sem, self.used, self.flying = sem, 0, {}

    def start(self, name, src, dst):
        copy = pltpu.make_async_copy(src, dst, self.sem.at[self.used])
        copy.start()
        self.used += 1
        self.flying[name] = copy

    def wait(self, name):
        self.flying.pop(name).wait()


def halve(arrays):
    rows, scen = arrays[0].shape
    width = scen // HALVES

    def body(*refs):
        for i in range(len(arrays)):
            for h in range(HALVES):
                refs[len(arrays) + HALVES * i + h][...] = refs[i][:, h * width : (h + 1) * width]

    many = HALVES * len(arrays)
    out = call(body, "halve", tuple(arrays), [VMEM] * len(arrays), [f32(rows, width)] * many, [VMEM] * many)
    return [out[HALVES * i : HALVES * (i + 1)] for i in range(len(arrays))]


def prepare(region, target, owned, kkt, cost, dual, cons, peers):
    blocks = target.shape[1]
    arrays = (kkt, cost, dual, cons)
    cuts = (CUTS, 1, 1, 1)

    def body(region_ref, target_hbm, *refs):
        from_refs, table_ref, to_refs, target_ref, sem = refs[:4], refs[4], refs[5:9], refs[9], refs[10]
        loads = Loads(sem)
        loads.start("target", target_hbm, target_ref)
        for i, (src, dst) in enumerate(zip(from_refs, to_refs)):
            size = src.shape[0] // cuts[i]
            for c in range(cuts[i]):
                at = slice(c * size, (c + 1) * size)
                loads.start((i, c), src.at[at, :], dst.at[at, :])
        here = ring_place(region_ref[0], peers)
        for i in range(2 * CAP * peers):
            table_ref[i] = -1
        loads.wait("target")
        for j in range(blocks):
            t = target_ref[0, j]

            @pl.when(t >= 0)
            def _(t=t, j=j):
                owner = t // owned
                ahead = ring_place(owner, peers) - here
                ahead = jnp.where(ahead < 0, ahead + peers, ahead)
                first = CAP * ahead
                at = first + jnp.where(table_ref[first] >= 0, 1, 0)
                table_ref[at] = j
                table_ref[CAP * peers + at] = t - owner * owned

        for i in range(4):
            for c in range(cuts[i]):
                loads.wait((i, c))

    out = call(
        body,
        "prepare",
        (region, target, *arrays),
        [SMEM] + [HBM] * 5,
        [jax.ShapeDtypeStruct((2 * CAP * peers,), jnp.int32)] + [jax.ShapeDtypeStruct(x.shape, x.dtype) for x in arrays],
        [SMEM] + [VMEM] * 4,
        [pltpu.SMEM(target.shape, jnp.int32), pltpu.SemaphoreType.DMA((1 + sum(cuts),))],
        moved=12 << 20,
    )
    return out[0], out[1:]


def columns(ref, h):
    width = ref.shape[1] // HALVES
    return ref.at[:, h * width : (h + 1) * width]


def base_rows(i, step, kkt, cost):
    rows, scen = kkt.shape[0], cost.shape[1]

    def body(kkt_ref, cost_ref, out_ref):
        out_ref[...] = jnp.dot(
            kkt_ref[i * step : (i + 1) * step, :], cost_ref[...], preferred_element_type=jnp.float32
        )

    return call(
        body,
        "base_rows",
        (kkt, cost),
        [VMEM, VMEM],
        f32(step, scen),
        VMEM,
        flops=2 * step * rows * scen,
        moved=3 << 20,
    )


def slots_of(table_ref, peers, blocks):
    out = []
    for r in range(peers):
        row = []
        for c in range(CAP):
            j = table_ref[CAP * r + c]
            b = table_ref[CAP * peers + CAP * r + c]
            read = jnp.maximum(j, 0)
            write = jnp.where(j < 0, blocks, j)
            row.append([pl.ds(pl.multiple_of(x * BLOCK, BLOCK), BLOCK) for x in (read, write, jnp.maximum(b, 0))] + [b])
        out.append(row)
    return out


def fold(x):
    return jnp.sum(x.reshape(-1, TILE, x.shape[-1]), axis=0)


def place(part_ref, totals, slots, owned):
    for o in range(owned):
        value = None
        for total, (_, _, _, b) in zip(totals, slots):
            mine = jnp.where(b == o, total, 0.0)
            value = mine if value is None else value + mine
        part_ref[o * BLOCK : (o + 1) * BLOCK, :] = value


def first_solve(h, table, pieces, dual, bases, kkt, owned, counting):
    peers = len(pieces)
    bound, scen = dual.shape
    width = scen // HALVES
    cols = slice(h * width, (h + 1) * width)
    own = owned * BLOCK
    sent = own + (TILE if counting else 0)
    step = bases[0].shape[0]
    chunks = bound // step

    def body(*refs):
        table_ref, refs = refs[0], refs[1:]
        piece, (dual_ref, kkt_ref), refs = refs[:peers], refs[peers : peers + 2], refs[peers + 2 :]
        piece = [ref if ref.shape[1] == width else columns(ref, h) for ref in piece]
        base_refs, z_ref, refs = refs[:chunks], refs[chunks], refs[chunks + 1 :]
        part, (drive_ref,) = refs[:peers], refs[peers:]
        slots = slots_of(table_ref, peers, bound // BLOCK)
        drive_ref[...] = jnp.zeros_like(drive_ref)
        for r in range(peers):
            for read, write, block, _ in slots[r]:
                drive_ref[write, :] = (penalty * (piece[r][block, :] - dual_ref[read, cols])).astype(jnp.bfloat16)
        for i in range(chunks * 2):
            half = step // 2
            at = slice(i * half, (i + 1) * half)
            here = slice(i % 2 * half, (i % 2 + 1) * half)
            got = jnp.dot(kkt_ref[at, :bound], drive_ref[:bound, :], preferred_element_type=jnp.float32)
            z_ref[at, :] = (base_refs[i // 2][here, cols] + got) + dual_ref[at, cols]
        for r in range(peers):
            place(part[r], [z_ref[read, :] for read, _, _, _ in slots[r]], slots[r], owned)
            if counting:
                row = lax.broadcasted_iota(jnp.int32, (TILE, width), 0)
                count = jnp.zeros((TILE, width), jnp.float32)
                for _, _, _, b in slots[r]:
                    count = count + jnp.where(row == b, 1.0, 0.0)
                part[r][own:, :] = count

    out = call(
        body,
        "first_solve",
        (table, *pieces, dual, kkt, *bases[:chunks]),
        [SMEM] + [VMEM] * (peers + 2 + chunks),
        [f32(bound, width)] + [f32(sent, width)] * peers,
        [VMEM] * (1 + peers),
        [pltpu.VMEM((bound + BLOCK, width), jnp.bfloat16)],
        flops=2 * bound * bound * width,
        moved=8 << 20,
    )
    return out[0], out[1:]


def second_solve(h, table, pieces, z, dual, bases, kkt, owned):
    peers = len(pieces)
    bound, scen = dual.shape
    step = bases[0].shape[0]
    chunks = bound // step
    width = scen // HALVES
    cols = slice(h * width, (h + 1) * width)
    own = owned * BLOCK

    def body(*refs):
        table_ref, refs = refs[0], refs[1:]
        piece, (z_ref, dual_ref, kkt_ref), refs = refs[:peers], refs[peers : peers + 3], refs[peers + 3 :]
        base_refs, refs = refs[:chunks], refs[chunks:]
        field_ref, drive_ref, next_ref, norm_ref, part = refs[0], refs[1], refs[2], refs[3], refs[4:]
        slots = slots_of(table_ref, peers, bound // BLOCK)
        drive_ref[...] = jnp.zeros_like(drive_ref)
        next_ref[:bound, :] = dual_ref[:, cols]
        gaps = jnp.zeros((TILE, width), jnp.float32)
        for r in range(peers):
            for read, write, block, b in slots[r]:
                fetched = piece[r][block, :]
                renewed_dual = z_ref[read, :] - fetched
                gap = renewed_dual - dual_ref[read, cols]
                gaps = gaps + jnp.where(b < 0, 0.0, fold(gap * gap))
                next_ref[write, :] = renewed_dual
                drive_ref[write, :] = (penalty * (fetched - renewed_dual)).astype(jnp.bfloat16)
        for i in range(chunks * 2):
            half = step // 2
            at = slice(i * half, (i + 1) * half)
            here = slice(i % 2 * half, (i % 2 + 1) * half)
            got = jnp.dot(kkt_ref[at, :bound], drive_ref[:bound, :], preferred_element_type=jnp.float32)
            field_ref[at, :] = base_refs[i // 2][here, cols] + got
        shifts = jnp.zeros((TILE, width), jnp.float32)
        for r in range(peers):
            totals = []
            for read, write, block, b in slots[r]:
                copies = field_ref[read, :]
                shift = copies - piece[r][block, :]
                shifts = shifts + jnp.where(b < 0, 0.0, fold(shift * shift))
                totals.append(copies + next_ref[read, :])
            for total, (_, write, _, _) in zip(totals, slots[r]):
                next_ref[write, :] = total
            place(part[r], totals, slots[r], owned)
        norm_ref[:TILE, :] = gaps
        norm_ref[TILE:, :] = shifts

    out = call(
        body,
        "second_solve",
        (table, *pieces, z, dual, kkt, *bases[:chunks]),
        [SMEM] + [VMEM] * (peers + 3 + chunks),
        [
            f32(bound, width),
            jax.ShapeDtypeStruct((bound + BLOCK, width), jnp.bfloat16),
            f32(bound + BLOCK, width),
            f32(2 * TILE, width),
        ]
        + [f32(own, width)] * peers,
        [VMEM] * (4 + peers),
        flops=2 * bound * bound * width,
        moved=8 << 20,
    )
    return out[0], out[1], out[2], out[3], out[4:]


def store_state(fields, drives, bases, kkt):
    bound, width = fields[0].shape
    rows = kkt.shape[0]
    step = bases[0].shape[0]
    rest = bases[bound // step :]

    def body(*refs):
        field_refs, drive_refs, kkt_ref, refs = refs[:HALVES], refs[HALVES : 2 * HALVES], refs[2 * HALVES], refs[2 * HALVES + 1 :]
        base_refs, (state_hbm, rest_ref, sem) = refs[: len(rest)], refs[len(rest) :]
        loads = Loads(sem)
        for h in range(HALVES):
            cols = slice(h * width, (h + 1) * width)
            loads.start(h, field_refs[h], state_hbm.at[:bound, cols])
        for h in range(HALVES):
            cols = slice(h * width, (h + 1) * width)
            for i in range(len(rest)):
                at = slice(i * step, (i + 1) * step)
                there = slice(bound + i * step, bound + (i + 1) * step)
                got = jnp.dot(kkt_ref[there, :bound], drive_refs[h][:bound, :], preferred_element_type=jnp.float32)
                rest_ref[at, cols] = base_refs[i][:, cols] + got
        loads.start("rest", rest_ref, state_hbm.at[bound:, :])
        for h in range(HALVES):
            loads.wait(h)
        loads.wait("rest")

    return call(
        body,
        "store_state",
        (*fields, *drives, kkt, *rest),
        [VMEM] * (2 * HALVES + 1 + len(rest)),
        f32(rows, HALVES * width),
        HBM,
        [pltpu.VMEM((rows - bound, HALVES * width), jnp.float32), pltpu.SemaphoreType.DMA((HALVES + 1,))],
        flops=2 * bound * (rows - bound) * HALVES * width,
        moved=4 << 20,
    )


def add_pairs(pairs):
    def body(*refs):
        for i in range(len(pairs)):
            refs[2 * len(pairs) + i][...] = refs[2 * i][...] + refs[2 * i + 1][...]

    out = call(
        body,
        "add_pairs",
        tuple(x for pair in pairs for x in pair),
        [VMEM] * (2 * len(pairs)),
        [f32(*pair[0].shape) for pair in pairs],
        [VMEM] * len(pairs),
    )
    return list(out)


def renew(h, parts, before, count, norms):
    own, width = before.shape[0], parts[0].shape[1]
    owned = own // BLOCK
    counted = count is None

    def body(*refs):
        parts_ref, refs = refs[: len(parts)], refs[len(parts) :]
        before_ref, refs = refs[0] if before.shape[1] == width else columns(refs[0], h), refs[1:]
        if not counted:
            count_ref, refs = refs[0], refs[1:]
        norm_refs, refs = refs[: len(norms)], refs[len(norms) :]
        new_ref, moved_ref = refs[0], refs[1]

        def total(at):
            value = parts_ref[0][at, :]
            for ref in parts_ref[1:]:
                value = value + ref[at, :]
            return value

        if counted:
            tile = total(slice(own, own + TILE))
            refs[2][...] = tile
        else:
            tile = count_ref[...]
        moved = jnp.zeros((TILE, width), jnp.float32)
        for b in range(owned):
            at = slice(b * BLOCK, (b + 1) * BLOCK)
            many = tile[b : b + 1, :]
            value = total(at) / jnp.maximum(many, 1.0)
            change = value - before_ref[at, :]
            moved = moved + many * fold(change * change)
            new_ref[at, :] = value
        moved_ref[...] = moved
        if norms:
            gaps = norm_refs[0][...] + norm_refs[3][...]
            sums = [
                gaps[:TILE, :],
                norm_refs[1][...] + norm_refs[4][...],
                gaps[TILE:, :],
                norm_refs[2][...] + moved,
            ]
            row = lax.broadcasted_iota(jnp.int32, (TILE, width), 0)
            block = jnp.zeros((TILE, width), jnp.float32)
            for i, x in enumerate(sums):
                block = jnp.where(row == i, jnp.sum(x, axis=0, keepdims=True), block)
            new_ref[own:, :] = block

    ins = (*parts, before) + (() if counted else (count,)) + tuple(norms)
    outs = [f32(own + (TILE if norms else 0), width), f32(TILE, width)] + ([f32(TILE, width)] if counted else [])
    return call(body, "renew", ins, [VMEM] * len(ins), outs, [VMEM] * len(outs))


def finish(table, pieces, zs, owned):
    peers = len(pieces[0])
    bound, width = zs[0].shape[0] - BLOCK, zs[0].shape[1]
    own = owned * BLOCK

    def body(*refs):
        table_ref, refs = refs[0], refs[1:]
        halves, refs = [refs[h * peers : (h + 1) * peers] for h in range(HALVES)], refs[HALVES * peers :]
        z_refs, (dual_hbm, cons_hbm, dual_ref, sem) = refs[:HALVES], refs[HALVES:]
        loads = Loads(sem)
        slots = slots_of(table_ref, peers, bound // BLOCK)
        for h in range(HALVES):
            cols = slice(h * width, (h + 1) * width)
            loads.start(("cons", h), halves[h][0].at[:own, :], cons_hbm.at[:, cols])
            dual_ref[:bound, cols] = z_refs[h][:bound, :]
            for r in range(peers):
                for read, write, block, _ in slots[r]:
                    dual_ref[write, cols] = z_refs[h][read, :] - halves[h][r][block, :]
        loads.start("dual", dual_ref.at[:bound, :], dual_hbm)
        for name in list(loads.flying):
            loads.wait(name)

    scen = HALVES * width
    return call(
        body,
        "finish",
        (table, *[piece for half in pieces for piece in half], *zs),
        [SMEM] + [VMEM] * (HALVES * (peers + 1)),
        [f32(bound, scen), f32(own, scen)],
        [HBM] * 2,
        [pltpu.VMEM((bound + BLOCK, scen), jnp.float32), pltpu.SemaphoreType.DMA((1 + HALVES,))],
        moved=3 << 20,
        room=14,
    )


def sum_tails(pieces, own, done):
    peers, width = len(pieces), pieces[0].shape[1]

    def body(*refs):
        total = refs[0][own:, :]
        for ref in refs[1:peers]:
            total = total + ref[own:, :]
        refs[-1][...] = total

    ins = (*pieces, *done)
    return call(body, "sum_tails", ins, [VMEM] * peers + [HBM] * len(done), f32(TILE, width), VMEM)


def norm_table(tiles, scale):
    def body(*refs):
        total = refs[0][...]
        for ref in refs[1:-1]:
            total = total + ref[...]
        total = jnp.sum(total, axis=1, keepdims=True)
        row = lax.broadcasted_iota(jnp.int32, (ITERS, 2), 0)
        col = lax.broadcasted_iota(jnp.int32, (ITERS, 2), 1)
        primal = jnp.where(row == 0, total[0:1, :], total[2:3, :] - total[3:4, :])
        moved = penalty * penalty * jnp.where(row == 0, total[1:2, :], total[3:4, :])
        refs[-1][...] = jnp.sqrt(jnp.maximum(jnp.where(col == 0, primal, moved), 0.0) / scale)

    return call(body, "norm_table", tuple(tiles), [VMEM] * len(tiles), f32(ITERS, 2), VMEM)


def shards(kkt, cost, dual, cons, target):
    scen = cost.shape[1]
    owned = cons.shape[0] // BLOCK
    peers = lax.axis_size("region")
    subs = lax.axis_size("sub")
    order = sorted(range(peers), key=lambda region: ring_place(region, peers))
    ahead = [(order[i], order[(i + 1) % peers]) for i in range(peers)]
    behind = [(b, a) for a, b in ahead]

    def forward(x):
        return lax.ppermute(x, "region", ahead)

    def backward(x):
        return lax.ppermute(x, "region", behind)

    def reach(h):
        long, short = peers // 2, (peers - 1) // 2
        return (long, short)

    def gather(h, piece, beside=lambda k, x: x, came=None):
        far, near = reach(h)
        pieces = [piece] * peers
        f = b = piece
        if came:
            f, b = pieces[peers - 1], pieces[1] = came
        for k in range(2 if came else 1, max(far, near) + 1):
            values = yield ([f] if k <= far else []) + ([b] if k <= near else [])
            values = beside(k, values)
            if k <= far:
                f = pieces[(peers - k) % peers] = forward(values.pop(0))
            if k <= near:
                b = pieces[k] = backward(values.pop(0))
        return pieces

    def scatter(h, parts):
        far, near = reach(h)
        f, b = parts[far], parts[peers - near]
        for k in range(1, max(far, near) + 1):
            going, coming = f, b
            values = yield ([f] if k <= far else []) + ([b] if k <= near else [])
            f = forward(values.pop(0)) if k <= far else going
            b = backward(values.pop(0)) if k <= near else coming
            pairs = []
            if k < far:
                pairs.append((f, parts[far - k]))
            if k < near:
                pairs.append((b, parts[peers - near + k]))
            if pairs:
                added = [add_pairs([pair])[0] for pair in pairs]
                if k < far:
                    f = added.pop(0)
                if k < near:
                    b = added.pop(0)
        return [parts[0], f, b]

    region = lax.axis_index("region").astype(jnp.int32).reshape(1)
    firsts = halve([forward(cons), backward(cons)])
    table, (kkt, cost, dual, own) = prepare(region, target, owned, kkt, cost, dual, cons, peers)
    step = math.gcd(dual.shape[0], kkt.shape[0])
    chunks = kkt.shape[0] // step
    bases = []

    def beside(h, k, values):
        turn = HALVES * (k - 1) + h
        some = [dual] if turn == LOAD_TURN else []
        while len(bases) < min(chunks, BASE_AT.get(turn, 0)):
            bases.append(base_rows(len(bases), step, kkt, cost))
            some.append(bases[-1])
        return tie(values, [], some) if some else values

    known = {"count": None, "norms": [], "solved": [], "last": []}

    def half(h):
        last = h == HALVES - 1
        pieces = yield from gather(h, own, lambda k, values: beside(h, k, values), [halves[h] for halves in firsts])
        z, parts = first_solve(h, table, pieces, dual, bases, kkt, owned, h == 0)
        arrived = yield from scatter(h, parts)
        out = renew(h, arrived, own, known["count"], ())
        averages, moved = out[0], out[1]
        if known["count"] is None:
            known["count"] = out[2]
        pieces = yield from gather(h, averages)
        field, drive, z, gaps, parts = second_solve(h, table, pieces, z, dual, bases, kkt, owned)
        known["solved"].append((field, drive))
        arrived = yield from scatter(h, parts)
        norms = known["norms"] + [gaps, moved]
        out = renew(h, arrived, averages, known["count"], norms if last else ())
        known["norms"] = norms + [out[1]]
        pieces = yield from gather(h, out[0])
        known["last"].append((pieces, z))

    turns = [half(h) for h in range(HALVES)]
    waiting = [next(turn) for turn in turns]
    which = LEAD * [0]
    while any(w is not None for w in waiting):
        h = which.pop(0) if which else next_turn(waiting, h)
        values = list(waiting[h])
        try:
            waiting[h] = turns[h].send(values)
        except StopIteration:
            waiting[h] = None
    fields, drives = zip(*known["solved"])
    state = store_state(fields, drives, bases, kkt)
    pieces, zs = zip(*known["last"])
    tail = sum_tails(pieces[-1], owned * BLOCK, [state])
    turned = [lax.ppermute(tail, "sub", [(i, i ^ k) for i in range(subs)]) for k in range(1, subs)]
    norms = norm_table([tail, *turned], float(peers * subs * scen * BLOCK))
    return (state, *finish(table, pieces, zs, owned), norms)


def next_turn(waiting, h):
    for k in range(1, len(waiting) + 1):
        if waiting[(h + k) % len(waiting)] is not None:
            return (h + k) % len(waiting)


def solution(mesh):
    spec = P(("region", "sub"), None)
    return jax.shard_map(
        shards, mesh=mesh, in_specs=(spec,) * 5, out_specs=(spec, spec, spec, P()), check_vma=False
    )
```

```python
import math

import jax
import jax.numpy as jnp
from jax import lax
from jax.experimental import pallas as pl
from jax.experimental.pallas import tpu as pltpu
from jax.sharding import PartitionSpec as P

BLOCK = 128
CAP = 2
ITERS = 2
HALVES = 2
TILE = 8
LEAD = 1
LOAD_TURN = 2
BASE_AT = {3: 2, 5: 4}
CUTS = 8


penalty = 1.5

VMEM = pl.BlockSpec(memory_space=pltpu.VMEM)
SMEM = pl.BlockSpec(memory_space=pltpu.SMEM)
HBM = pl.BlockSpec(memory_space=pltpu.HBM)


def grid_of(peers):
    columns = 1
    while (2 * columns) ** 2 <= peers:
        columns *= 2
    return peers // columns, columns


def ring_place(region, peers):
    rows, columns = grid_of(peers)
    row, column = region // columns, region % columns
    up = rows - 1 - row
    if columns == 1:
        return row
    right = up % 2 == 0
    if isinstance(region, int):
        if column == 0:
            return row
        return rows + up * (columns - 1) + (column - 1 if right else columns - 1 - column)
    along = jnp.where(right, column - 1, columns - 1 - column)
    return jnp.where(column == 0, row, rows + up * (columns - 1) + along)


def f32(*shape):
    return jax.ShapeDtypeStruct(shape, jnp.float32)


def call(body, name, ins, in_specs, outs, out_specs, scratch=(), aliases=None, flops=0, moved=1 << 20, room=4, pins=()):
    ins = tuple(pltpu.with_memory_space_constraint(x, pltpu.HBM) if spec is HBM else x for x, spec in zip(ins, in_specs))
    many = isinstance(outs, (list, tuple))
    shapes, specs = (list(outs), list(out_specs)) if many else ([outs], [out_specs])
    for i, spec in enumerate(specs):
        if spec is HBM:
            shapes[i] = pltpu.HBM(shapes[i].shape, shapes[i].dtype)
        elif i in pins:
            shapes[i] = pltpu.VMEM(shapes[i].shape, shapes[i].dtype)
    return pl.pallas_call(
        body,
        name=name,
        out_shape=shapes if many else shapes[0],
        in_specs=in_specs,
        out_specs=out_specs,
        scratch_shapes=scratch,
        input_output_aliases=aliases or {},
        cost_estimate=pl.CostEstimate(flops=flops, bytes_accessed=moved, transcendentals=0),
        compiler_params=pltpu.CompilerParams(vmem_limit_bytes=room << 20),
    )(*ins)


def tie(values, others, near=()):
    values, others = list(values), list(others)

    def body(*refs):
        del refs

    out = call(
        body,
        "tie",
        (*values, *others, *near),
        [VMEM] * len(values) + [HBM] * len(others) + [VMEM] * len(near),
        [f32(*x.shape) for x in values],
        [VMEM] * len(values),
        aliases={i: i for i in range(len(values))},
        moved=0,
    )
    return list(out)


class Loads:
    def __init__(self, sem):
        self.sem, self.used, self.flying = sem, 0, {}

    def start(self, name, src, dst):
        copy = pltpu.make_async_copy(src, dst, self.sem.at[self.used])
        copy.start()
        self.used += 1
        self.flying[name] = copy

    def wait(self, name):
        self.flying.pop(name).wait()


def halve(arrays):
    rows, scen = arrays[0].shape
    width = scen // HALVES

    def body(*refs):
        for i in range(len(arrays)):
            for h in range(HALVES):
                refs[len(arrays) + HALVES * i + h][...] = refs[i][:, h * width : (h + 1) * width]

    many = HALVES * len(arrays)
    out = call(body, "halve", tuple(arrays), [VMEM] * len(arrays), [f32(rows, width)] * many, [VMEM] * many)
    return [out[HALVES * i : HALVES * (i + 1)] for i in range(len(arrays))]


def prepare(region, target, owned, kkt, cost, dual, cons, peers):
    blocks = target.shape[1]
    arrays = (kkt, cost, dual, cons)
    cuts = (CUTS, 1, 1, 1)

    def body(region_ref, target_hbm, *refs):
        from_refs, table_ref, to_refs, target_ref, sem = refs[:4], refs[4], refs[5:9], refs[9], refs[10]
        loads = Loads(sem)
        loads.start("target", target_hbm, target_ref)
        for i, (src, dst) in enumerate(zip(from_refs, to_refs)):
            size = src.shape[0] // cuts[i]
            for c in range(cuts[i]):
                at = slice(c * size, (c + 1) * size)
                loads.start((i, c), src.at[at, :], dst.at[at, :])
        here = ring_place(region_ref[0], peers)
        for i in range(2 * CAP * peers):
            table_ref[i] = -1
        loads.wait("target")
        for j in range(blocks):
            t = target_ref[0, j]

            @pl.when(t >= 0)
            def _(t=t, j=j):
                owner = t // owned
                ahead = ring_place(owner, peers) - here
                ahead = jnp.where(ahead < 0, ahead + peers, ahead)
                first = CAP * ahead
                at = first + jnp.where(table_ref[first] >= 0, 1, 0)
                table_ref[at] = j
                table_ref[CAP * peers + at] = t - owner * owned

        for i in range(4):
            for c in range(cuts[i]):
                loads.wait((i, c))

    out = call(
        body,
        "prepare",
        (region, target, *arrays),
        [SMEM] + [HBM] * 5,
        [jax.ShapeDtypeStruct((2 * CAP * peers,), jnp.int32)] + [jax.ShapeDtypeStruct(x.shape, x.dtype) for x in arrays],
        [SMEM] + [VMEM] * 4,
        [pltpu.SMEM(target.shape, jnp.int32), pltpu.SemaphoreType.DMA((1 + sum(cuts),))],
        moved=12 << 20,
    )
    return out[0], out[1:]


def columns(ref, h):
    width = ref.shape[1] // HALVES
    return ref.at[:, h * width : (h + 1) * width]


def base_rows(i, step, kkt, cost):
    rows, scen = kkt.shape[0], cost.shape[1]

    def body(kkt_ref, cost_ref, out_ref):
        out_ref[...] = jnp.dot(
            kkt_ref[i * step : (i + 1) * step, :], cost_ref[...], preferred_element_type=jnp.float32
        )

    return call(
        body,
        "base_rows",
        (kkt, cost),
        [VMEM, VMEM],
        f32(step, scen),
        VMEM,
        flops=2 * step * rows * scen,
        moved=3 << 20,
    )


def slots_of(table_ref, peers, blocks):
    out = []
    for r in range(peers):
        row = []
        for c in range(CAP):
            j = table_ref[CAP * r + c]
            b = table_ref[CAP * peers + CAP * r + c]
            read = jnp.maximum(j, 0)
            write = jnp.where(j < 0, blocks, j)
            row.append([pl.ds(pl.multiple_of(x * BLOCK, BLOCK), BLOCK) for x in (read, write, jnp.maximum(b, 0))] + [b])
        out.append(row)
    return out


def fold(x):
    return jnp.sum(x.reshape(-1, TILE, x.shape[-1]), axis=0)


def place(part_ref, totals, slots, owned):
    for o in range(owned):
        value = None
        for total, (_, _, _, b) in zip(totals, slots):
            mine = jnp.where(b == o, total, 0.0)
            value = mine if value is None else value + mine
        part_ref[o * BLOCK : (o + 1) * BLOCK, :] = value


def first_solve(h, table, pieces, dual, bases, kkt, owned, counting):
    peers = len(pieces)
    bound, scen = dual.shape
    width = scen // HALVES
    cols = slice(h * width, (h + 1) * width)
    own = owned * BLOCK
    sent = own + (TILE if counting else 0)
    step = bases[0].shape[0]
    chunks = bound // step

    def body(*refs):
        table_ref, refs = refs[0], refs[1:]
        piece, (dual_ref, kkt_ref), refs = refs[:peers], refs[peers : peers + 2], refs[peers + 2 :]
        piece = [ref if ref.shape[1] == width else columns(ref, h) for ref in piece]
        base_refs, z_ref, refs = refs[:chunks], refs[chunks], refs[chunks + 1 :]
        part, (drive_ref,) = refs[:peers], refs[peers:]
        slots = slots_of(table_ref, peers, bound // BLOCK)
        drive_ref[...] = jnp.zeros_like(drive_ref)
        for r in range(peers):
            for read, write, block, _ in slots[r]:
                drive_ref[write, :] = (penalty * (piece[r][block, :] - dual_ref[read, cols])).astype(jnp.bfloat16)
        for i in range(chunks * 2):
            half = step // 2
            at = slice(i * half, (i + 1) * half)
            here = slice(i % 2 * half, (i % 2 + 1) * half)
            got = jnp.dot(kkt_ref[at, :bound], drive_ref[:bound, :], preferred_element_type=jnp.float32)
            z_ref[at, :] = (base_refs[i // 2][here, cols] + got) + dual_ref[at, cols]
        for r in range(peers):
            place(part[r], [z_ref[read, :] for read, _, _, _ in slots[r]], slots[r], owned)
            if counting:
                row = lax.broadcasted_iota(jnp.int32, (TILE, width), 0)
                count = jnp.zeros((TILE, width), jnp.float32)
                for _, _, _, b in slots[r]:
                    count = count + jnp.where(row == b, 1.0, 0.0)
                part[r][own:, :] = count

    out = call(
        body,
        "first_solve",
        (table, *pieces, dual, kkt, *bases[:chunks]),
        [SMEM] + [VMEM] * (peers + 2 + chunks),
        [f32(bound, width)] + [f32(sent, width)] * peers,
        [VMEM] * (1 + peers),
        [pltpu.VMEM((bound + BLOCK, width), jnp.bfloat16)],
        flops=2 * bound * bound * width,
        moved=8 << 20,
    )
    return out[0], out[1:]


def second_solve(h, table, pieces, z, dual, bases, kkt, owned):
    peers = len(pieces)
    bound, scen = dual.shape
    step = bases[0].shape[0]
    chunks = bound // step
    width = scen // HALVES
    cols = slice(h * width, (h + 1) * width)
    own = owned * BLOCK

    def body(*refs):
        table_ref, refs = refs[0], refs[1:]
        piece, (z_ref, dual_ref, kkt_ref), refs = refs[:peers], refs[peers : peers + 3], refs[peers + 3 :]
        base_refs, refs = refs[:chunks], refs[chunks:]
        field_ref, drive_ref, next_ref, norm_ref, part = refs[0], refs[1], refs[2], refs[3], refs[4:]
        slots = slots_of(table_ref, peers, bound // BLOCK)
        drive_ref[...] = jnp.zeros_like(drive_ref)
        next_ref[:bound, :] = dual_ref[:, cols]
        gaps = jnp.zeros((TILE, width), jnp.float32)
        for r in range(peers):
            for read, write, block, b in slots[r]:
                fetched = piece[r][block, :]
                renewed_dual = z_ref[read, :] - fetched
                gap = renewed_dual - dual_ref[read, cols]
                gaps = gaps + jnp.where(b < 0, 0.0, fold(gap * gap))
                next_ref[write, :] = renewed_dual
                drive_ref[write, :] = (penalty * (fetched - renewed_dual)).astype(jnp.bfloat16)
        for i in range(chunks * 2):
            half = step // 2
            at = slice(i * half, (i + 1) * half)
            here = slice(i % 2 * half, (i % 2 + 1) * half)
            got = jnp.dot(kkt_ref[at, :bound], drive_ref[:bound, :], preferred_element_type=jnp.float32)
            field_ref[at, :] = base_refs[i // 2][here, cols] + got
        shifts = jnp.zeros((TILE, width), jnp.float32)
        for r in range(peers):
            totals = []
            for read, write, block, b in slots[r]:
                copies = field_ref[read, :]
                shift = copies - piece[r][block, :]
                shifts = shifts + jnp.where(b < 0, 0.0, fold(shift * shift))
                totals.append(copies + next_ref[read, :])
            for total, (_, write, _, _) in zip(totals, slots[r]):
                next_ref[write, :] = total
            place(part[r], totals, slots[r], owned)
        norm_ref[:TILE, :] = gaps
        norm_ref[TILE:, :] = shifts

    out = call(
        body,
        "second_solve",
        (table, *pieces, z, dual, kkt, *bases[:chunks]),
        [SMEM] + [VMEM] * (peers + 3 + chunks),
        [
            f32(bound, width),
            jax.ShapeDtypeStruct((bound + BLOCK, width), jnp.bfloat16),
            f32(bound + BLOCK, width),
            f32(2 * TILE, width),
        ]
        + [f32(own, width)] * peers,
        [VMEM] * (4 + peers),
        flops=2 * bound * bound * width,
        moved=8 << 20,
    )
    return out[0], out[1], out[2], out[3], out[4:]


def store_state(fields, drives, bases, kkt):
    bound, width = fields[0].shape
    rows = kkt.shape[0]
    step = bases[0].shape[0]
    rest = bases[bound // step :]

    def body(*refs):
        field_refs, drive_refs, kkt_ref, refs = refs[:HALVES], refs[HALVES : 2 * HALVES], refs[2 * HALVES], refs[2 * HALVES + 1 :]
        base_refs, (state_hbm, rest_ref, sem) = refs[: len(rest)], refs[len(rest) :]
        loads = Loads(sem)
        for h in range(HALVES):
            cols = slice(h * width, (h + 1) * width)
            loads.start(h, field_refs[h], state_hbm.at[:bound, cols])
        for h in range(HALVES):
            cols = slice(h * width, (h + 1) * width)
            for i in range(len(rest)):
                at = slice(i * step, (i + 1) * step)
                there = slice(bound + i * step, bound + (i + 1) * step)
                got = jnp.dot(kkt_ref[there, :bound], drive_refs[h][:bound, :], preferred_element_type=jnp.float32)
                rest_ref[at, cols] = base_refs[i][:, cols] + got
        loads.start("rest", rest_ref, state_hbm.at[bound:, :])
        for h in range(HALVES):
            loads.wait(h)
        loads.wait("rest")

    return call(
        body,
        "store_state",
        (*fields, *drives, kkt, *rest),
        [VMEM] * (2 * HALVES + 1 + len(rest)),
        f32(rows, HALVES * width),
        HBM,
        [pltpu.VMEM((rows - bound, HALVES * width), jnp.float32), pltpu.SemaphoreType.DMA((HALVES + 1,))],
        flops=2 * bound * (rows - bound) * HALVES * width,
        moved=4 << 20,
    )


def add_pairs(pairs):
    def body(*refs):
        for i in range(len(pairs)):
            refs[2 * len(pairs) + i][...] = refs[2 * i][...] + refs[2 * i + 1][...]

    out = call(
        body,
        "add_pairs",
        tuple(x for pair in pairs for x in pair),
        [VMEM] * (2 * len(pairs)),
        [f32(*pair[0].shape) for pair in pairs],
        [VMEM] * len(pairs),
    )
    return list(out)


def renew(h, parts, before, count, norms):
    own, width = before.shape[0], parts[0].shape[1]
    owned = own // BLOCK
    counted = count is None

    def body(*refs):
        parts_ref, refs = refs[: len(parts)], refs[len(parts) :]
        before_ref, refs = refs[0] if before.shape[1] == width else columns(refs[0], h), refs[1:]
        if not counted:
            count_ref, refs = refs[0], refs[1:]
        norm_refs, refs = refs[: len(norms)], refs[len(norms) :]
        new_ref, moved_ref = refs[0], refs[1]

        def total(at):
            value = parts_ref[0][at, :]
            for ref in parts_ref[1:]:
                value = value + ref[at, :]
            return value

        if counted:
            tile = total(slice(own, own + TILE))
            refs[2][...] = tile
        else:
            tile = count_ref[...]
        moved = jnp.zeros((TILE, width), jnp.float32)
        for b in range(owned):
            at = slice(b * BLOCK, (b + 1) * BLOCK)
            many = tile[b : b + 1, :]
            value = total(at) / jnp.maximum(many, 1.0)
            change = value - before_ref[at, :]
            moved = moved + many * fold(change * change)
            new_ref[at, :] = value
        moved_ref[...] = moved
        if norms:
            gaps = norm_refs[0][...] + norm_refs[3][...]
            sums = [
                gaps[:TILE, :],
                norm_refs[1][...] + norm_refs[4][...],
                gaps[TILE:, :],
                norm_refs[2][...] + moved,
            ]
            row = lax.broadcasted_iota(jnp.int32, (TILE, width), 0)
            block = jnp.zeros((TILE, width), jnp.float32)
            for i, x in enumerate(sums):
                block = jnp.where(row == i, jnp.sum(x, axis=0, keepdims=True), block)
            new_ref[own:, :] = block

    ins = (*parts, before) + (() if counted else (count,)) + tuple(norms)
    outs = [f32(own + (TILE if norms else 0), width), f32(TILE, width)] + ([f32(TILE, width)] if counted else [])
    return call(body, "renew", ins, [VMEM] * len(ins), outs, [VMEM] * len(outs))


def finish(table, pieces, zs, owned):
    peers = len(pieces[0])
    bound, width = zs[0].shape[0] - BLOCK, zs[0].shape[1]
    own = owned * BLOCK

    def body(*refs):
        table_ref, refs = refs[0], refs[1:]
        halves, refs = [refs[h * peers : (h + 1) * peers] for h in range(HALVES)], refs[HALVES * peers :]
        z_refs, (dual_hbm, cons_hbm, dual_ref, sem) = refs[:HALVES], refs[HALVES:]
        loads = Loads(sem)
        slots = slots_of(table_ref, peers, bound // BLOCK)
        for h in range(HALVES):
            cols = slice(h * width, (h + 1) * width)
            loads.start(("cons", h), halves[h][0].at[:own, :], cons_hbm.at[:, cols])
            dual_ref[:bound, cols] = z_refs[h][:bound, :]
            for r in range(peers):
                for read, write, block, _ in slots[r]:
                    dual_ref[write, cols] = z_refs[h][read, :] - halves[h][r][block, :]
        loads.start("dual", dual_ref.at[:bound, :], dual_hbm)
        for name in list(loads.flying):
            loads.wait(name)

    scen = HALVES * width
    return call(
        body,
        "finish",
        (table, *[piece for half in pieces for piece in half], *zs),
        [SMEM] + [VMEM] * (HALVES * (peers + 1)),
        [f32(bound, scen), f32(own, scen)],
        [HBM] * 2,
        [pltpu.VMEM((bound + BLOCK, scen), jnp.float32), pltpu.SemaphoreType.DMA((1 + HALVES,))],
        moved=3 << 20,
        room=14,
    )


def sum_tails(pieces, own, done):
    peers, width = len(pieces), pieces[0].shape[1]

    def body(*refs):
        total = refs[0][own:, :]
        for ref in refs[1:peers]:
            total = total + ref[own:, :]
        refs[-1][...] = total

    ins = (*pieces, *done)
    return call(body, "sum_tails", ins, [VMEM] * peers + [HBM] * len(done), f32(TILE, width), VMEM)


def norm_table(tiles, scale):
    def body(*refs):
        total = refs[0][...]
        for ref in refs[1:-1]:
            total = total + ref[...]
        total = jnp.sum(total, axis=1, keepdims=True)
        row = lax.broadcasted_iota(jnp.int32, (ITERS, 2), 0)
        col = lax.broadcasted_iota(jnp.int32, (ITERS, 2), 1)
        primal = jnp.where(row == 0, total[0:1, :], total[2:3, :] - total[3:4, :])
        moved = penalty * penalty * jnp.where(row == 0, total[1:2, :], total[3:4, :])
        refs[-1][...] = jnp.sqrt(jnp.maximum(jnp.where(col == 0, primal, moved), 0.0) / scale)

    return call(body, "norm_table", tuple(tiles), [VMEM] * len(tiles), f32(ITERS, 2), VMEM)


def shards(kkt, cost, dual, cons, target):
    scen = cost.shape[1]
    owned = cons.shape[0] // BLOCK
    peers = lax.axis_size("region")
    subs = lax.axis_size("sub")
    order = sorted(range(peers), key=lambda region: ring_place(region, peers))
    ahead = [(order[i], order[(i + 1) % peers]) for i in range(peers)]
    behind = [(b, a) for a, b in ahead]

    def forward(x):
        return lax.ppermute(x, "region", ahead)

    def backward(x):
        return lax.ppermute(x, "region", behind)

    def reach(h):
        long, short = peers // 2, (peers - 1) // 2
        return (long, short)

    def gather(h, piece, beside=lambda k, x: x, came=None):
        far, near = reach(h)
        pieces = [piece] * peers
        f = b = piece
        if came:
            f, b = pieces[peers - 1], pieces[1] = came
        for k in range(2 if came else 1, max(far, near) + 1):
            values = yield ([f] if k <= far else []) + ([b] if k <= near else [])
            values = beside(k, values)
            if k <= far:
                f = pieces[(peers - k) % peers] = forward(values.pop(0))
            if k <= near:
                b = pieces[k] = backward(values.pop(0))
        return pieces

    def scatter(h, parts):
        far, near = reach(h)
        f, b = parts[far], parts[peers - near]
        for k in range(1, max(far, near) + 1):
            going, coming = f, b
            values = yield ([f] if k <= far else []) + ([b] if k <= near else [])
            f = forward(values.pop(0)) if k <= far else going
            b = backward(values.pop(0)) if k <= near else coming
            pairs = []
            if k < far:
                pairs.append((f, parts[far - k]))
            if k < near:
                pairs.append((b, parts[peers - near + k]))
            if pairs:
                added = [add_pairs([pair])[0] for pair in pairs]
                if k < far:
                    f = added.pop(0)
                if k < near:
                    b = added.pop(0)
        return [parts[0], f, b]

    region = lax.axis_index("region").astype(jnp.int32).reshape(1)
    firsts = halve([forward(cons), backward(cons)])
    table, (kkt, cost, dual, own) = prepare(region, target, owned, kkt, cost, dual, cons, peers)
    step = math.gcd(dual.shape[0], kkt.shape[0])
    chunks = kkt.shape[0] // step
    bases = []

    def beside(h, k, values):
        turn = HALVES * (k - 1) + h
        some = [dual] if turn == LOAD_TURN else []
        while len(bases) < min(chunks, BASE_AT.get(turn, 0)):
            bases.append(base_rows(len(bases), step, kkt, cost))
            some.append(bases[-1])
        return tie(values, [], some) if some else values

    known = {"count": None, "norms": [], "solved": [], "last": []}

    def half(h):
        last = h == HALVES - 1
        pieces = yield from gather(h, own, lambda k, values: beside(h, k, values), [halves[h] for halves in firsts])
        z, parts = first_solve(h, table, pieces, dual, bases, kkt, owned, h == 0)
        arrived = yield from scatter(h, parts)
        out = renew(h, arrived, own, known["count"], ())
        averages, moved = out[0], out[1]
        if known["count"] is None:
            known["count"] = out[2]
        pieces = yield from gather(h, averages)
        field, drive, z, gaps, parts = second_solve(h, table, pieces, z, dual, bases, kkt, owned)
        known["solved"].append((field, drive))
        arrived = yield from scatter(h, parts)
        norms = known["norms"] + [gaps, moved]
        out = renew(h, arrived, averages, known["count"], norms if last else ())
        known["norms"] = norms + [out[1]]
        pieces = yield from gather(h, out[0])
        known["last"].append((pieces, z))

    turns = [half(h) for h in range(HALVES)]
    waiting = [next(turn) for turn in turns]
    which = LEAD * [0]
    while any(w is not None for w in waiting):
        h = which.pop(0) if which else next_turn(waiting, h)
        values = list(waiting[h])
        try:
            waiting[h] = turns[h].send(values)
        except StopIteration:
            waiting[h] = None
    fields, drives = zip(*known["solved"])
    state = store_state(fields, drives, bases, kkt)
    pieces, zs = zip(*known["last"])
    tail = sum_tails(pieces[-1], owned * BLOCK, [state])
    turned = [lax.ppermute(tail, "sub", [(i, i ^ k) for i in range(subs)]) for k in range(1, subs)]
    norms = norm_table([tail, *turned], float(peers * subs * scen * BLOCK))
    return (state, *finish(table, pieces, zs, owned), norms)


def next_turn(waiting, h):
    for k in range(1, len(waiting) + 1):
        if waiting[(h + k) % len(waiting)] is not None:
            return (h + k) % len(waiting)


def solution(mesh):
    spec = P(("region", "sub"), None)
    return jax.shard_map(
        shards, mesh=mesh, in_specs=(spec,) * 5, out_specs=(spec, spec, spec, P()), check_vma=False
    )
```
